32 devices in a mesh: ctx: 8 (over z, x), ch: 4 (over y, core).
Axes of the slice: x: 2, y: 2, z: 4, core: 2. Of those that a mesh axis runs over, the one named last changes fastest.
Arguments:
- gate_q: bfloat16 [3072, 4096], P('ctx', 'ch'), may hold values from -6 to 6
- key_k: bfloat16 [3072, 4096], P('ctx', 'ch'), may hold values from -6 to 6
- value_v: bfloat16 [3072, 4096], P('ctx', 'ch'), may hold values from -6 to 6
- long_filter: bfloat16 [3072, 4096], P('ctx', 'ch'), may hold values from -0.109375 to 0.109375
- skip_gain: float32 [4096], P('ch'), may hold values from 0.5 to 1.5
- out_weight: bfloat16 [4096, 4096], P('ch'), may hold values from -0.125 to 0.125
Outputs:
- mixed: bfloat16 [3072, 4096], P('ctx', 'ch')
The draws below stay inside these ranges and needn't reach their ends.
All inputs are finite; a program needn't handle non-finite values.
Results may differ from the reference program's by a relative error of at most 0.023.
Values may be sent and summed in bfloat16 or wider, within the bound.
No kernel may reach another device: no remote copies, remote signals or barrier semaphores. Data moves between devices by JAX's collectives and lax.ppermute only.
A program may use at most 128 MiB of HBM per device.

```python
import jax
import jax.numpy as jnp
from jax import lax

D = 4096
TOKENS = 3072
N_CH = 4


def spiked(entries, own_key, source, target, parts, factor):
    owner, partner = [(jnp.arange(entries.shape[dim]) // (entries.shape[dim] // parts)).reshape([-1 if axis == dim else 1 for axis in range(entries.ndim)]) for dim in (source, target)]
    chosen = jax.random.permutation(own_key, parts)[partner]
    strong = (owner == chosen) | (owner == (partner + parts // 2) % parts)
    return jnp.where(strong, factor * entries, entries)


def block_levels(rng, shape, shards, low, top_value):
    loudness, own = 1.0, jax.random.fold_in(rng, 6)
    for axis_at, shards_of in shards:
        heights = jnp.exp(jax.random.uniform(jax.random.fold_in(own, axis_at), (shards_of,), jnp.float32, low / len(shards), top_value / len(shards)))
        loudness = loudness * jnp.repeat(heights, shape[axis_at] // shards_of).reshape([-1 if axis == axis_at else 1 for axis in range(len(shape))])
    return loudness


def centred(own_key, extent, deviation, most, shards=(), held_as=jnp.bfloat16):
    drawn = deviation * jax.random.normal(own_key, extent, jnp.float32)
    if shards:
        drawn = drawn * block_levels(own_key, extent, shards, -0.22, 0.18)
    return jnp.clip(drawn, -most, most).astype(held_as)


def gaussian_with(rng, extent, scale, most, split, heavy, dtype=jnp.bfloat16):
    entries = scale * jax.random.normal(rng, extent, jnp.float32)
    if split:
        entries = entries * block_levels(rng, extent, split, -0.22, 0.18)
    return jnp.clip(spiked(entries, jax.random.fold_in(rng, 3), *heavy), -most, most).astype(dtype)


def setup_inputs(seed: int = 0) -> dict:
    key_of = jax.random.split(jax.random.key(seed), 7)
    gate_q = centred(key_of[0], (TOKENS, D), 1.0, 6.0, ((0, 8), (1, 4)))
    key_k = centred(key_of[1], (TOKENS, D), 1.0, 6.0, ((0, 8), (1, 4)))
    value_v = centred(key_of[2], (TOKENS, D), 1.0, 6.0, ((0, 8), (1, 4)))
    long_filter = centred(key_of[3], (TOKENS, D), TOKENS ** -0.5, 0.109375, ((0, 8), (1, 4)))
    skip_gain = jnp.clip(0.5 + 1.0 * jax.random.uniform(key_of[4], (D,), jnp.float32) ** block_levels(key_of[4], (D,), ((0, 4),), -0.2, 0.2), 0.5, 1.5)
    out_weight = gaussian_with(key_of[5], (D, D), D ** -0.5, 0.125, ((0, 4),), (0, 1, 4, 2.0))
    return dict(gate_q=gate_q, key_k=key_k, value_v=value_v, long_filter=long_filter, skip_gain=skip_gain, out_weight=out_weight)


def reference(gate_q, key_k, value_v, long_filter, skip_gain, out_weight):
    width = D // N_CH
    total = jnp.zeros((TOKENS, D), jnp.float32)
    for group in range(N_CH):
        first = group * width
        gated = (key_k[:, first:first + width].astype(jnp.float32) * value_v[:, first:first + width].astype(jnp.float32)).astype(jnp.bfloat16)
        gated_full = gated.astype(jnp.float32)
        taps = long_filter[:, first:first + width].astype(jnp.float32)
        spectrum = jnp.fft.rfft(gated_full, n=2 * TOKENS, axis=0) * jnp.fft.rfft(taps, n=2 * TOKENS, axis=0)
        conv = jnp.fft.irfft(spectrum, n=2 * TOKENS, axis=0)[:TOKENS].astype(jnp.float32)
        hidden = (gate_q[:, first:first + width].astype(jnp.float32) * (conv + skip_gain[first:first + width][None, :] * gated_full)).astype(jnp.bfloat16)
        partial_value = jnp.dot(hidden, out_weight[first:first + width, :], preferred_element_type=jnp.float32).astype(jnp.bfloat16)
        partial_value = lax.optimization_barrier(partial_value)
        total = total + partial_value.astype(jnp.float32)
    return total.astype(jnp.bfloat16)
```

```python
import functools
import math

import jax
import jax.numpy as jnp
import numpy as np
from jax import lax
from jax.experimental import pallas as pl
from jax.experimental.pallas import tpu as pltpu
from jax.sharding import PartitionSpec as P

F32 = jnp.float32
BF16 = jnp.bfloat16
VMEM = pl.BlockSpec(memory_space=pltpu.VMEM)
SMEM = pl.BlockSpec(memory_space=pltpu.SMEM)
SUB = 8
PARAMS = pltpu.CompilerParams(vmem_limit_bytes=56 * 2**20)


def tables(total, inner):
    outer = total // inner
    n1 = np.arange(outer)
    eye = np.eye(SUB)
    ang = 2.0 * np.pi * np.outer(n1 + 0.25, n1) / outer
    first = np.stack([np.cos(ang), -np.sin(ang)], axis=1)
    first = np.einsum("kcn,ij->kcinj", first, eye).reshape(2 * outer * SUB, outer * SUB)
    last = np.stack([np.cos(ang), -np.sin(ang)], axis=1) / total
    last = np.einsum("kcn,ij->nikcj", last, eye).reshape(outer * SUB, 2 * outer * SUB)
    n2 = np.arange(inner)
    freq = n1[:, None] + outer * n2[None, :] + 0.25
    ang = 2.0 * np.pi * freq[:, :, None] * n2[None, None, :] / total
    cos, sin = np.cos(ang), np.sin(ang)
    mid = np.concatenate(
        [np.concatenate([cos, sin], axis=2), np.concatenate([-sin, cos], axis=2)], axis=1
    )
    back = np.swapaxes(mid, 1, 2)
    return tuple(jnp.asarray(np.ascontiguousarray(a).astype(jnp.bfloat16)) for a in (first, mid, back, last))


def slices_kernel(idx_ref, *refs, ins, count, width):
    arrays, outs = refs[:ins], refs[ins:]
    me = idx_ref[0]
    for s in range(count):
        at = pl.ds(pl.multiple_of(lax.rem(me + s, count) * width, width), width)
        if ins == 1:
            outs[s][...] = arrays[0][:, at]
        else:
            outs[s][...] = (arrays[0][:, at].astype(F32) * arrays[1][:, at].astype(F32)).astype(BF16)


def send_slices(idx, arrays, count):
    rows, channels = arrays[0].shape
    width = channels // count
    if width % 128:
        value = arrays[0]
        if len(arrays) == 2:
            value = (arrays[0].astype(F32) * arrays[1].astype(F32)).astype(BF16)
        return [
            lax.dynamic_slice_in_dim(value, lax.rem(idx[0] + s, count) * width, width, 1)
            for s in range(count)
        ]
    return pl.pallas_call(
        functools.partial(slices_kernel, ins=len(arrays), count=count, width=width),
        out_shape=[jax.ShapeDtypeStruct((rows, width), BF16)] * count,
        in_specs=[SMEM] + [VMEM] * len(arrays),
        out_specs=[VMEM] * count,
        compiler_params=PARAMS,
        cost_estimate=pl.CostEstimate(flops=rows * channels, bytes_accessed=4 * rows * channels, transcendentals=0),
    )(idx, *arrays)


def exchange(blocks, axis, count):
    out = [blocks[0]]
    for s in range(1, count):
        out.append(lax.ppermute(blocks[s], axis, [(i, (i + s) % count) for i in range(count)]))
    return out


def gather_positions(me, blocks, spot, count):
    outer_here = blocks[0].shape[0] // spot.shape[1]
    for s in range(count):
        src = lax.rem(me + count - s, count)
        spot[pl.ds(src * outer_here, outer_here)] = blocks[s][...].reshape(outer_here, *spot.shape[1:])


def halves(tile):
    tile = tile.astype(F32)
    width = tile.shape[-1]
    return [
        tile[..., at : at + SUB, :].reshape(-1, width).astype(BF16) for at in (0, SUB)
    ]


def forward_first(first_ref, spot, mixed):
    outer, inner, width = spot.shape

    def body(i, carry):
        rows = pl.ds(pl.multiple_of(i * 2 * SUB, 2 * SUB), 2 * SUB)
        parts = [
            jnp.dot(first_ref[...], part, preferred_element_type=F32).reshape(outer, 2, SUB, width)
            for part in halves(spot[:, rows, :])
        ]
        mixed[:, :, rows, :] = jnp.concatenate(parts, axis=2).astype(BF16)
        return carry

    lax.fori_loop(0, inner // (2 * SUB), body, 0)


def filter_kernel(idx_ref, first_ref, mid_ref, *refs, count):
    blocks, (out_ref, spot, mixed) = refs[:count], refs[count:]
    gather_positions(idx_ref[0], blocks, spot, count)
    forward_first(first_ref, spot, mixed)
    outer, _, inner, width = mixed.shape

    def body(k, carry):
        out_ref[k] = jnp.dot(
            mid_ref[k], mixed[k].reshape(2 * inner, width), preferred_element_type=F32
        ).astype(BF16)
        return carry

    lax.fori_loop(0, outer, body, 0)


def conv_kernel(idx_ref, first_ref, mid_ref, back_ref, last_ref, filt_ref, *refs, count):
    blocks, outs, (spot, mixed) = refs[:count], refs[count : 2 * count], refs[2 * count :]
    me = idx_ref[0]
    gather_positions(me, blocks, spot, count)
    forward_first(first_ref, spot, mixed)
    outer, _, inner, width = mixed.shape

    def middle(k, carry):
        spec = jnp.dot(mid_ref[k], mixed[k].reshape(2 * inner, width), preferred_element_type=F32)
        filt = filt_ref[k].astype(F32)
        re, im = spec[:inner], spec[inner:]
        fre, fim = filt[:inner], filt[inner:]
        prod = jnp.concatenate([re * fre - im * fim, re * fim + im * fre], axis=0).astype(BF16)
        turned = jnp.dot(back_ref[k], prod, preferred_element_type=F32)
        mixed[k] = turned.astype(BF16).reshape(2, inner, width)
        return carry

    lax.fori_loop(0, outer, middle, 0)

    def ending(i, carry):
        rows = pl.ds(pl.multiple_of(i * 2 * SUB, 2 * SUB), 2 * SUB)
        parts = [
            jnp.dot(last_ref[...], part, preferred_element_type=F32).reshape(outer, SUB, width)
            for part in halves(mixed[:, :, rows, :])
        ]
        spot[:, rows, :] = jnp.concatenate(parts, axis=1).astype(BF16)
        return carry

    lax.fori_loop(0, inner // (2 * SUB), ending, 0)
    here = outer // count
    for s in range(count):
        dst = lax.rem(me + s, count)
        outs[s][...] = spot[pl.ds(dst * here, here)].reshape(here * inner, width)


def hidden_kernel(idx_ref, gate_ref, key_ref, value_ref, gain_ref, *refs, count):
    blocks, out_ref = refs[:count], refs[count]
    me = idx_ref[0]
    width = blocks[0].shape[1]
    for s in range(count):
        src = lax.rem(me + count - s, count)
        at = pl.ds(pl.multiple_of(src * width, width), width)
        gated = (key_ref[:, at].astype(F32) * value_ref[:, at].astype(F32)).astype(BF16).astype(F32)
        total = blocks[s][...].astype(F32) + gain_ref[:, at] * gated
        out_ref[:, at] = (gate_ref[:, at].astype(F32) * total).astype(BF16)


def make_hidden(idx, gate_q, key_k, value_v, gain, blocks):
    count = len(blocks)
    rows, channels = gate_q.shape
    width = channels // count
    if width % 128:
        conv = jnp.zeros((rows, channels), F32)
        for s in range(count):
            src = lax.rem(idx[0] + count - s, count)
            conv = lax.dynamic_update_slice_in_dim(conv, blocks[s].astype(F32), src * width, 1)
        gated = (key_k.astype(F32) * value_v.astype(F32)).astype(BF16).astype(F32)
        return (gate_q.astype(F32) * (conv + gain * gated)).astype(BF16)
    return pl.pallas_call(
        functools.partial(hidden_kernel, count=count),
        out_shape=jax.ShapeDtypeStruct((rows, channels), BF16),
        in_specs=[SMEM] + [VMEM] * (4 + count),
        out_specs=VMEM,
        compiler_params=PARAMS,
    )(idx, gate_q, key_k, value_v, gain, *blocks)


def project_kernel(group_ref, hid_ref, weight_ref, *refs):
    value = jnp.dot(hid_ref[...], weight_ref[...], preferred_element_type=F32)
    if len(refs) == 2:
        value = value + refs[0][...].astype(F32)
    refs[-1][...] = value.astype(refs[-1].dtype)


def project(hidden, weight, group, groups, extra=None, dtype=BF16):
    rows, channels = hidden.shape
    width = weight.shape[1] // groups
    tile = min(512, width)
    steps = width // tile
    specs = [
        pl.BlockSpec((rows, channels), lambda j, g: (0, 0)),
        pl.BlockSpec((channels, tile), lambda j, g: (0, g[0] * steps + j)),
    ]
    args = [hidden, weight]
    if extra is not None:
        specs.append(pl.BlockSpec((rows, tile), lambda j, g: (0, j)))
        args.append(extra)
    return pl.pallas_call(
        project_kernel,
        out_shape=jax.ShapeDtypeStruct((rows, width), dtype),
        grid_spec=pltpu.PrefetchScalarGridSpec(
            num_scalar_prefetch=1,
            grid=(steps,),
            in_specs=specs,
            out_specs=pl.BlockSpec((rows, tile), lambda j, g: (0, j)),
        ),
        compiler_params=PARAMS,
        cost_estimate=pl.CostEstimate(
            flops=2 * rows * channels * width, bytes_accessed=2 * channels * width, transcendentals=0
        ),
    )(group, *args)


def local(gate_q, key_k, value_v, long_filter, skip_gain, out_weight):
    rows, channels = key_k.shape
    count = lax.axis_size("ctx")
    groups = lax.axis_size("ch")
    chips = groups // 2
    total = rows * count
    inner = next(n for n in range(128, 0, -16) if rows % n == 0)
    outer = total // inner
    width = channels // count
    idx = lax.axis_index("ctx").astype(jnp.int32).reshape(1)
    first, mid, back, last = tables(total, inner)
    spot = pltpu.VMEM((outer, inner, width), BF16)
    mixed = pltpu.VMEM((outer, 2, inner, width), BF16)

    filter_in = exchange(send_slices(idx, [long_filter], count), "ctx", count)
    gated_in = exchange(send_slices(idx, [key_k, value_v], count), "ctx", count)
    spectrum = pl.pallas_call(
        functools.partial(filter_kernel, count=count),
        out_shape=jax.ShapeDtypeStruct((outer, 2 * inner, width), BF16),
        in_specs=[SMEM] + [VMEM] * (2 + count),
        out_specs=VMEM,
        scratch_shapes=[spot, mixed],
        compiler_params=PARAMS,
        cost_estimate=pl.CostEstimate(flops=3 * 10**9, bytes_accessed=8 * 10**6, transcendentals=0),
    )(idx, first, mid, *filter_in)
    conv_out = pl.pallas_call(
        functools.partial(conv_kernel, count=count),
        out_shape=[jax.ShapeDtypeStruct((rows, width), BF16)] * count,
        in_specs=[SMEM] + [VMEM] * (5 + count),
        out_specs=[VMEM] * count,
        scratch_shapes=[spot, mixed],
        compiler_params=PARAMS,
        cost_estimate=pl.CostEstimate(flops=6 * 10**9, bytes_accessed=12 * 10**6, transcendentals=0),
    )(idx, first, mid, back, last, spectrum, *gated_in)
    conv_in = exchange(conv_out, "ctx", count)
    hidden = make_hidden(idx, gate_q, key_k, value_v, skip_gain[None, :], conv_in)

    here = lax.axis_index("ch").astype(jnp.int32)
    chip, core = here // 2, here % 2
    swap = [(i, i ^ 1) for i in range(groups)]

    def group_of(step, which):
        return (lax.rem(chip + step, chips) * 2 + which).reshape(1)

    steps = list(range(1, chips)) + [0]
    crossed = [
        lax.ppermute(project(hidden, out_weight, group_of(step, 1 - core), groups), "ch", swap) for step in steps
    ]
    arrived = []
    for step, extra in zip(steps[:-1], crossed[:-1]):
        part = project(hidden, out_weight, group_of(step, core), groups, extra)
        arrived.append(lax.ppermute(part, "ch", [(i, (i + 2 * step) % groups) for i in range(groups)]))
    result = project(hidden, out_weight, group_of(0, core), groups, crossed[-1], F32)
    for part in arrived:
        result = result + part.astype(F32)
    return result.astype(BF16)


def solution(mesh):
    placed = (
        P("ctx", "ch"),
        P("ctx", "ch"),
        P("ctx", "ch"),
        P("ctx", "ch"),
        P("ch"),
        P("ch", None),
    )
    return jax.shard_map(
        local, mesh=mesh, in_specs=placed, out_specs=P("ctx", "ch"), check_vma=False
    )
```

```python
import functools
import math

import jax
import jax.numpy as jnp
import numpy as np
from jax import lax
from jax.experimental import pallas as pl
from jax.experimental.pallas import tpu as pltpu
from jax.sharding import PartitionSpec as P

F32 = jnp.float32
BF16 = jnp.bfloat16
VMEM = pl.BlockSpec(memory_space=pltpu.VMEM)
SMEM = pl.BlockSpec(memory_space=pltpu.SMEM)
HBM = pl.BlockSpec(memory_space=pltpu.HBM)
SUB = 8


def params(nbytes):
    return pltpu.CompilerParams(vmem_limit_bytes=int(min(nbytes + 8 * 2**20, 58 * 2**20)))


def tables(total, inner):
    outer = total // inner
    n1 = np.arange(outer)
    eye = np.eye(SUB)
    ang = 2.0 * np.pi * np.outer(n1 + 0.25, n1) / outer
    first = np.stack([np.cos(ang), -np.sin(ang)], axis=1)
    first = np.einsum("kcn,ij->kcinj", first, eye).reshape(2 * outer * SUB, outer * SUB)
    last = np.stack([np.cos(ang), -np.sin(ang)], axis=1) / total
    last = np.einsum("kcn,ij->nikcj", last, eye).reshape(outer * SUB, 2 * outer * SUB)
    n2 = np.arange(inner)
    freq = n1[:, None] + outer * n2[None, :] + 0.25
    ang = 2.0 * np.pi * freq[:, :, None] * n2[None, None, :] / total
    cos, sin = np.cos(ang), np.sin(ang)
    mid = np.concatenate(
        [np.concatenate([cos, sin], axis=2), np.concatenate([-sin, cos], axis=2)], axis=1
    )
    back = np.swapaxes(mid, 1, 2)
    return tuple(jnp.asarray(np.ascontiguousarray(a).astype(jnp.bfloat16)) for a in (first, mid, back, last))


def split_kernel(idx_ref, array_ref, *refs, count):
    *outs, sems = refs
    width = outs[0].shape[1]
    copies = []
    for s in range(count):
        at = pl.ds(pl.multiple_of(lax.rem(idx_ref[0] + s, count) * width, width), width)
        copies.append(pltpu.make_async_copy(array_ref.at[:, at], outs[s], sems.at[s]))
        copies[-1].start()
    for copy in copies:
        copy.wait()


def gate_kernel(idx_ref, key_ref, value_ref, *outs, count):
    width = outs[0].shape[1]
    for s in range(count):
        at = pl.ds(pl.multiple_of(lax.rem(idx_ref[0] + s, count) * width, width), width)
        outs[s][...] = (key_ref[:, at].astype(F32) * value_ref[:, at].astype(F32)).astype(BF16)


def send_slices(idx, arrays, count):
    rows, channels = arrays[0].shape
    width = channels // count
    if width % 128:
        value = arrays[0]
        if len(arrays) == 2:
            value = (arrays[0].astype(F32) * arrays[1].astype(F32)).astype(BF16)
        return [
            lax.dynamic_slice_in_dim(value, lax.rem(idx[0] + s, count) * width, width, 1)
            for s in range(count)
        ]
    alone = len(arrays) == 1
    if alone:
        arrays = [pltpu.with_memory_space_constraint(arrays[0], pltpu.HBM)]
    return pl.pallas_call(
        functools.partial(split_kernel if alone else gate_kernel, count=count),
        out_shape=[jax.ShapeDtypeStruct((rows, width), BF16)] * count,
        in_specs=[SMEM] + ([HBM] if alone else [VMEM] * 2),
        out_specs=[VMEM] * count,
        scratch_shapes=[pltpu.SemaphoreType.DMA((count,))] if alone else [],
        compiler_params=params(2 * (len(arrays) + 1) * rows * channels),
        cost_estimate=pl.CostEstimate(flops=rows * channels, bytes_accessed=4 * rows * channels, transcendentals=0),
    )(idx, *arrays)


def exchange(blocks, axis, count):
    out = [blocks[0]]
    for s in range(1, count):
        out.append(lax.ppermute(blocks[s], axis, [(i, (i + s) % count) for i in range(count)]))
    return out


def gather_positions(me, blocks, spot, count):
    outer_here = blocks[0].shape[0] // spot.shape[1]
    for s in range(count):
        src = lax.rem(me + count - s, count)
        spot[pl.ds(src * outer_here, outer_here)] = blocks[s][...].reshape(outer_here, *spot.shape[1:])


def halves(tile):
    tile = tile.astype(F32)
    width = tile.shape[-1]
    return jnp.concatenate(
        [tile[..., at : at + SUB, :].reshape(-1, width).astype(BF16) for at in (0, SUB)], axis=1
    )


def joined(value, lead):
    width = value.shape[1] // 2
    parts = [value[:, at : at + width].reshape(*lead, SUB, width) for at in (0, width)]
    return jnp.concatenate(parts, axis=len(lead)).astype(BF16)


def for_each(count, body):
    if count <= 32:
        for i in range(count):
            body(i)
    else:
        lax.fori_loop(0, count, lambda i, c: (body(i), c)[1], 0, unroll=4 if count % 4 == 0 else 1)


def forward_first(first_ref, spot, mixed):
    outer, inner, _ = spot.shape

    def body(i):
        rows = pl.ds(i * 2 * SUB, 2 * SUB)
        value = jnp.dot(first_ref[...], halves(spot[:, rows, :]), preferred_element_type=F32)
        mixed[:, :, rows, :] = joined(value, (outer, 2))

    for_each(inner // (2 * SUB), body)


def filter_kernel(idx_ref, first_ref, mid_ref, *refs, count):
    blocks, (out_ref, spot, mixed) = refs[:count], refs[count:]
    gather_positions(idx_ref[0], blocks, spot, count)
    forward_first(first_ref, spot, mixed)
    outer, _, inner, width = mixed.shape

    def body(k):
        out_ref[k] = jnp.dot(
            mid_ref[k], mixed[k].reshape(2 * inner, width), preferred_element_type=F32
        ).astype(BF16)

    for_each(outer, body)


def conv_kernel(idx_ref, first_ref, mid_ref, back_ref, last_ref, filt_ref, *refs, count):
    blocks, outs, (spot, mixed) = refs[:count], refs[count : 2 * count], refs[2 * count :]
    me = idx_ref[0]
    gather_positions(me, blocks, spot, count)
    forward_first(first_ref, spot, mixed)
    outer, _, inner, width = mixed.shape

    def middle(k):
        spec = jnp.dot(mid_ref[k], mixed[k].reshape(2 * inner, width), preferred_element_type=F32)
        filt = filt_ref[k].astype(F32)
        re, im = spec[:inner], spec[inner:]
        fre, fim = filt[:inner], filt[inner:]
        prod = jnp.concatenate([re * fre - im * fim, re * fim + im * fre], axis=0).astype(BF16)
        turned = jnp.dot(back_ref[k], prod, preferred_element_type=F32)
        mixed[k] = turned.astype(BF16).reshape(2, inner, width)

    for_each(outer, middle)

    def ending(i):
        rows = pl.ds(i * 2 * SUB, 2 * SUB)
        value = jnp.dot(last_ref[...], halves(mixed[:, :, rows, :]), preferred_element_type=F32)
        spot[:, rows, :] = joined(value, (outer,))

    for_each(inner // (2 * SUB), ending)
    here = outer // count
    for s in range(count):
        dst = lax.rem(me + s, count)
        outs[s][...] = spot[pl.ds(dst * here, here)].reshape(here * inner, width)


def prepare_kernel(order_ref, key_ref, value_ref, gain_ref, weight_ref, skip_ref, *refs):
    *outs, sems = refs
    width = outs[0].shape[1]
    copies = []
    for j, out_ref in enumerate(outs):
        at = pl.ds(pl.multiple_of(order_ref[j] * width, width), width)
        copies.append(pltpu.make_async_copy(weight_ref.at[:, at], out_ref, sems.at[j]))
        copies[-1].start()
    gated = (key_ref[...].astype(F32) * value_ref[...].astype(F32)).astype(BF16).astype(F32)
    skip_ref[...] = gain_ref[...] * gated
    for copy in copies:
        copy.wait()


def prepare(order, key_k, value_v, gain, weight):
    groups = order.shape[0]
    width = weight.shape[1] // groups
    return pl.pallas_call(
        prepare_kernel,
        out_shape=[jax.ShapeDtypeStruct(key_k.shape, F32)]
        + [jax.ShapeDtypeStruct((weight.shape[0], width), BF16)] * groups,
        in_specs=[SMEM] + [VMEM] * 3 + [HBM],
        out_specs=[VMEM] * (1 + groups),
        scratch_shapes=[pltpu.SemaphoreType.DMA((groups,))],
        compiler_params=params(8 * key_k.size + 2 * weight.size),
        cost_estimate=pl.CostEstimate(flops=key_k.size, bytes_accessed=2 * weight.size, transcendentals=0),
    )(order, key_k, value_v, gain, pltpu.with_memory_space_constraint(weight, pltpu.HBM))


def hidden_kernel(idx_ref, gate_ref, skip_ref, weight_ref, *refs, count):
    blocks, out_ref, part_refs = refs[:count], refs[count], refs[count + 1 :]
    me = idx_ref[0]
    width = blocks[0].shape[1]
    for s in range(count):
        src = lax.rem(me + count - s, count)
        at = pl.ds(pl.multiple_of(src * width, width), width)
        total = blocks[s][...].astype(F32) + skip_ref[:, at]
        out_ref[:, at] = (gate_ref[:, at].astype(F32) * total).astype(BF16)
    times_columns(out_ref, weight_ref, part_refs)


def times_columns(hid_ref, weight_ref, part_refs, extra_refs=()):
    rows, width = part_refs[0].shape
    tile = min(256, width)
    for r, part_ref in enumerate(part_refs):
        for j in range(width // tile):
            cols = slice(j * tile, (j + 1) * tile)
            value = jnp.dot(
                hid_ref[r * rows : (r + 1) * rows, :], weight_ref[:, cols], preferred_element_type=F32
            )
            if extra_refs:
                value = value + extra_refs[r][:, cols].astype(F32)
            part_ref[:, cols] = value.astype(part_ref.dtype)


def project_kernel(hid_ref, weight_ref, *refs, extra):
    times_columns(hid_ref, weight_ref, refs[extra:], refs[:extra])


def project(hidden, weight, pieces, extra=(), dtype=BF16):
    rows, channels = hidden.shape
    width = weight.shape[1]
    return pl.pallas_call(
        functools.partial(project_kernel, extra=len(extra)),
        out_shape=[jax.ShapeDtypeStruct((rows // pieces, width), dtype)] * pieces,
        in_specs=[VMEM] * (2 + len(extra)),
        out_specs=[VMEM] * pieces,
        compiler_params=params(2 * channels * width + 2 * rows * channels + 10 * rows * width),
        cost_estimate=pl.CostEstimate(
            flops=2 * rows * channels * width, bytes_accessed=2 * channels * width, transcendentals=0
        ),
    )(hidden, weight, *extra)


def start_projection(idx, gate_q, skip, weight, blocks, pieces):
    count = len(blocks)
    rows, channels = gate_q.shape
    width = channels // count
    if width % 128:
        conv = jnp.zeros((rows, channels), F32)
        for s in range(count):
            src = lax.rem(idx[0] + count - s, count)
            conv = lax.dynamic_update_slice_in_dim(conv, blocks[s].astype(F32), src * width, 1)
        hidden = (gate_q.astype(F32) * (conv + skip)).astype(BF16)
        return hidden, project(hidden, weight, pieces)
    columns = weight.shape[1]
    hidden, *parts = pl.pallas_call(
        functools.partial(hidden_kernel, count=count),
        out_shape=[jax.ShapeDtypeStruct((rows, channels), BF16)]
        + [jax.ShapeDtypeStruct((rows // pieces, columns), BF16)] * pieces,
        in_specs=[SMEM] + [VMEM] * (3 + count),
        out_specs=[VMEM] * (1 + pieces),
        compiler_params=params(2 * channels * columns + 10 * rows * channels + 2 * rows * columns),
        cost_estimate=pl.CostEstimate(
            flops=2 * rows * channels * columns, bytes_accessed=2 * channels * columns, transcendentals=0
        ),
    )(idx, gate_q, skip, weight, *blocks)
    return hidden, parts


def finish_kernel(*refs, at, terms):
    values, (out_ref, held, sem) = refs[:terms], refs[-3:]
    total = values[0][...]
    for value in values[1:]:
        total = total + value[...].astype(F32)
    held[...] = total.astype(BF16)
    rows = held.shape[0]
    copy = pltpu.make_async_copy(held, out_ref.at[pl.ds(at, rows), :], sem)
    copy.start()
    copy.wait()


def finish(values, at, rows, buffer):
    here, columns = values[0].shape
    aliased = [] if buffer is None else [buffer]
    return pl.pallas_call(
        functools.partial(finish_kernel, at=at, terms=len(values)),
        out_shape=jax.ShapeDtypeStruct((rows, columns), BF16),
        in_specs=[VMEM] * len(values) + [HBM] * len(aliased),
        out_specs=HBM,
        scratch_shapes=[pltpu.VMEM((here, columns), BF16), pltpu.SemaphoreType.DMA],
        input_output_aliases={len(values): 0} if aliased else {},
        compiler_params=params(2 * here * columns * (len(values) + 2)),
    )(*values, *aliased)


def local(gate_q, key_k, value_v, long_filter, skip_gain, out_weight):
    rows, channels = key_k.shape
    count = lax.axis_size("ctx")
    groups = lax.axis_size("ch")
    chips = groups // 2
    total = rows * count
    inner = next(n for n in range(128, 0, -16) if rows % n == 0)
    outer = total // inner
    width = channels // count
    lanes = -(-width // 128) * 128
    idx = lax.axis_index("ctx").astype(jnp.int32).reshape(1)
    first, mid, back, last = tables(total, inner)
    spot = pltpu.VMEM((outer, inner, width), BF16)
    mixed = pltpu.VMEM((outer, 2, inner, width), BF16)
    signal = 2 * total * lanes
    table = 2 * (first.size + mid.size)

    filter_in = exchange(send_slices(idx, [long_filter], count), "ctx", count)
    gated_in = exchange(send_slices(idx, [key_k, value_v], count), "ctx", count)
    here = lax.axis_index("ch").astype(jnp.int32)
    chip, core = here // 2, here % 2
    steps = list(range(1, chips)) + [0]
    order = [lax.rem(chip + step, chips) * 2 + which for step in steps for which in (1 - core, core)]
    skip, *weights = prepare(jnp.stack(order), key_k, value_v, skip_gain[None, :], out_weight)
    spectrum = pl.pallas_call(
        functools.partial(filter_kernel, count=count),
        out_shape=jax.ShapeDtypeStruct((outer, 2 * inner, width), BF16),
        in_specs=[SMEM] + [VMEM] * (2 + count),
        out_specs=VMEM,
        scratch_shapes=[spot, mixed],
        compiler_params=params(table + 6 * signal),
        cost_estimate=pl.CostEstimate(flops=3 * 10**9, bytes_accessed=8 * 10**6, transcendentals=0),
    )(idx, first, mid, *filter_in)
    spectrum, skip, *weights = lax.optimization_barrier((spectrum, skip, *weights))
    conv_out = pl.pallas_call(
        functools.partial(conv_kernel, count=count),
        out_shape=[jax.ShapeDtypeStruct((rows, width), BF16)] * count,
        in_specs=[SMEM] + [VMEM] * (5 + count),
        out_specs=[VMEM] * count,
        scratch_shapes=[spot, mixed],
        compiler_params=params(2 * table + 7 * signal),
        cost_estimate=pl.CostEstimate(flops=6 * 10**9, bytes_accessed=12 * 10**6, transcendentals=0),
    )(idx, first, mid, back, last, spectrum, *gated_in)
    conv_in = exchange(conv_out, "ctx", count)

    swap = [(i, i ^ 1) for i in range(groups)]
    pieces = 2

    def to_core(parts):
        return [lax.ppermute(part, "ch", swap) for part in parts]

    hidden, parts = start_projection(idx, gate_q, skip, weights[0], conv_in, pieces)
    arrived = []
    for at, step in enumerate(steps[:-1]):
        if at:
            parts = project(hidden, weights[2 * at], pieces)
        crossed = to_core(parts)
        own = project(hidden, weights[2 * at + 1], pieces, dtype=F32)
        perm = [(i, (i + 2 * step) % groups) for i in range(groups)]
        arrived.append(
            [
                lax.ppermute((a + b.astype(F32)).astype(BF16), "ch", perm)
                for a, b in zip(own, crossed)
            ]
        )
    crossed = to_core(project(hidden, weights[-2], pieces))
    own = project(hidden, weights[-1], pieces, crossed, F32)
    result = None
    for r in range(pieces):
        result = finish([own[r]] + [parts[r] for parts in arrived], r * (rows // pieces), rows, result)
    return result


def solution(mesh):
    placed = (
        P("ctx", "ch"),
        P("ctx", "ch"),
        P("ctx", "ch"),
        P("ctx", "ch"),
        P("ch"),
        P("ch", None),
    )
    return jax.shard_map(
        local, mesh=mesh, in_specs=placed, out_specs=P("ctx", "ch"), check_vma=False
    )
```

```python
import functools
import math

import jax
import jax.numpy as jnp
import numpy as np
from jax import lax
from jax.experimental import pallas as pl
from jax.experimental.pallas import tpu as pltpu
from jax.sharding import PartitionSpec as P

F32 = jnp.float32
BF16 = jnp.bfloat16
VMEM = pl.BlockSpec(memory_space=pltpu.VMEM)
SMEM = pl.BlockSpec(memory_space=pltpu.SMEM)
HBM = pl.BlockSpec(memory_space=pltpu.HBM)
SUB = 8


def params(nbytes):
    return pltpu.CompilerParams(vmem_limit_bytes=int(min(nbytes + 4 * 2**20, 58 * 2**20)))


def tables(total, inner):
    outer = total // inner
    n1 = np.arange(outer)
    eye = np.eye(SUB)
    ang = 2.0 * np.pi * np.outer(n1 + 0.25, n1) / outer
    first = np.stack([np.cos(ang), -np.sin(ang)], axis=1)
    first = np.einsum("kcn,ij->kcinj", first, eye).reshape(2 * outer * SUB, outer * SUB)
    last = np.stack([np.cos(ang), -np.sin(ang)], axis=1) / total
    last = np.einsum("kcn,ij->nikcj", last, eye).reshape(outer * SUB, 2 * outer * SUB)
    n2 = np.arange(inner)
    freq = n1[:, None] + outer * n2[None, :] + 0.25
    ang = 2.0 * np.pi * freq[:, :, None] * n2[None, None, :] / total
    cos, sin = np.cos(ang), np.sin(ang)
    mid = np.concatenate(
        [np.concatenate([cos, sin], axis=2), np.concatenate([-sin, cos], axis=2)], axis=1
    )
    back = np.swapaxes(mid, 1, 2)
    return tuple(jnp.asarray(np.ascontiguousarray(a).astype(jnp.bfloat16)) for a in (first, mid, back, last))


def split_kernel(idx_ref, array_ref, *outs, count):
    width = outs[0].shape[1]
    for s in range(count):
        at = pl.ds(pl.multiple_of(lax.rem(idx_ref[0] + s, count) * width, width), width)
        outs[s][...] = array_ref[:, at]


def filter_slices(idx, value, count):
    rows, channels = value.shape
    width = channels // count
    if width % 128:
        return [
            lax.dynamic_slice_in_dim(value, lax.rem(idx[0] + s, count) * width, width, 1)
            for s in range(count)
        ]
    return pl.pallas_call(
        functools.partial(split_kernel, count=count),
        out_shape=[jax.ShapeDtypeStruct((rows, width), BF16)] * count,
        in_specs=[SMEM, VMEM],
        out_specs=[VMEM] * count,
        compiler_params=params(4 * rows * channels),
        cost_estimate=pl.CostEstimate(flops=0, bytes_accessed=4 * rows * channels, transcendentals=0),
    )(idx, value)


def gate_kernel(idx_ref, order_ref, key_hbm, value_hbm, weight_ref, *refs, count):
    outs, columns = refs[:count], refs[count:-4]
    key_ref, value_ref, own_sems, sems = refs[-4:]
    width, cols = outs[0].shape[1], columns[0].shape[1]
    copies = [
        pltpu.make_async_copy(key_hbm, key_ref, own_sems.at[0]),
        pltpu.make_async_copy(value_hbm, value_ref, own_sems.at[1]),
    ]
    for j, column_ref in enumerate(columns):
        at = pl.ds(pl.multiple_of(order_ref[j] * cols, cols), cols)
        copies.append(pltpu.make_async_copy(weight_ref.at[:, at], column_ref, sems.at[j]))
    for copy in copies:
        copy.start()
    for copy in copies[:2]:
        copy.wait()
    for s in range(count):
        at = pl.ds(pl.multiple_of(lax.rem(idx_ref[0] + s, count) * width, width), width)
        outs[s][...] = (key_ref[:, at].astype(F32) * value_ref[:, at].astype(F32)).astype(BF16)
    for copy in copies[2:]:
        copy.wait()


def plain_kernel(order_ref, weight_ref, *refs):
    *columns, sems = refs
    cols = columns[0].shape[1]
    copies = []
    for j, column_ref in enumerate(columns):
        at = pl.ds(pl.multiple_of(order_ref[j] * cols, cols), cols)
        copies.append(pltpu.make_async_copy(weight_ref.at[:, at], column_ref, sems.at[j]))
        copies[-1].start()
    for copy in copies:
        copy.wait()


def gated_slices(idx, key_k, value_v, count, order, weight, groups):
    rows, channels = key_k.shape
    width, cols = channels // count, weight.shape[1] // groups
    picked = order.shape[0]
    weight = pltpu.with_memory_space_constraint(weight, pltpu.HBM)
    columns = [pltpu.VMEM((weight.shape[0], cols), BF16)] * picked
    limit = 8 * rows * channels + 2 * picked * weight.shape[0] * cols
    cost = pl.CostEstimate(flops=rows * channels, bytes_accessed=limit, transcendentals=0)
    if width % 128:
        gated = (key_k.astype(F32) * value_v.astype(F32)).astype(BF16)
        return filter_slices(idx, gated, count), pl.pallas_call(
            plain_kernel,
            out_shape=columns,
            in_specs=[SMEM, HBM],
            out_specs=[VMEM] * picked,
            scratch_shapes=[pltpu.SemaphoreType.DMA((picked,))],
            compiler_params=params(limit),
            cost_estimate=cost,
        )(order, weight)
    outs = pl.pallas_call(
        functools.partial(gate_kernel, count=count),
        out_shape=[jax.ShapeDtypeStruct((rows, width), BF16)] * count + columns,
        in_specs=[SMEM, SMEM] + [HBM] * 3,
        out_specs=[VMEM] * (count + picked),
        scratch_shapes=[pltpu.VMEM((rows, channels), BF16)] * 2
        + [pltpu.SemaphoreType.DMA((2,)), pltpu.SemaphoreType.DMA((picked,))],
        compiler_params=params(limit),
        cost_estimate=cost,
    )(
        idx,
        order,
        pltpu.with_memory_space_constraint(key_k, pltpu.HBM),
        pltpu.with_memory_space_constraint(value_v, pltpu.HBM),
        weight,
    )
    return outs[:count], outs[count:]


def exchange(blocks, axis, count):
    out = [blocks[0]]
    for s in range(1, count):
        out.append(lax.ppermute(blocks[s], axis, [(i, (i + s) % count) for i in range(count)]))
    return out


def gather_positions(me, blocks, spot, count):
    outer_here = blocks[0].shape[0] // spot.shape[1]
    for s in range(count):
        src = lax.rem(me + count - s, count)
        spot[pl.ds(src * outer_here, outer_here)] = blocks[s][...].reshape(outer_here, *spot.shape[1:])


def halves(tile):
    tile = tile.astype(F32)
    width = tile.shape[-1]
    return jnp.concatenate(
        [tile[..., at : at + SUB, :].reshape(-1, width).astype(BF16) for at in (0, SUB)], axis=1
    )


def joined(value, lead):
    width = value.shape[1] // 2
    parts = [value[:, at : at + width].reshape(*lead, SUB, width) for at in (0, width)]
    return jnp.concatenate(parts, axis=len(lead)).astype(BF16)


def for_each(count, body):
    if count <= 32:
        for i in range(count):
            body(i)
    else:
        lax.fori_loop(0, count, lambda i, c: (body(i), c)[1], 0, unroll=4 if count % 4 == 0 else 1)


def forward_first(first_ref, spot, mixed):
    outer, inner, _ = spot.shape

    def body(i):
        rows = pl.ds(i * 2 * SUB, 2 * SUB)
        value = jnp.dot(first_ref[...], halves(spot[:, rows, :]), preferred_element_type=F32)
        mixed[:, :, rows, :] = joined(value, (outer, 2))

    for_each(inner // (2 * SUB), body)


def filter_kernel(idx_ref, first_ref, mid_hbm, back_hbm, *refs, count):
    blocks, (out_ref, mid_ref, back_ref, spot, mixed, sems) = refs[:count], refs[count:]
    outer, _, inner, width = mixed.shape
    parts = sems.shape[0] - 1
    cuts = [outer * p // parts for p in range(parts + 1)]
    spans = [pl.ds(lo, hi - lo) for lo, hi in zip(cuts, cuts[1:])]
    copies = [pltpu.make_async_copy(mid_hbm.at[at], mid_ref.at[at], sems.at[p]) for p, at in enumerate(spans)]
    copies.append(pltpu.make_async_copy(back_hbm, back_ref, sems.at[parts]))
    for copy in copies:
        copy.start()
    gather_positions(idx_ref[0], blocks, spot, count)
    forward_first(first_ref, spot, mixed)

    for p in range(parts):
        copies[p].wait()

        def body(k):
            k = k + cuts[p]
            out_ref[k] = jnp.dot(
                mid_ref[k], mixed[k].reshape(2 * inner, width), preferred_element_type=F32
            ).astype(BF16)

        for_each(cuts[p + 1] - cuts[p], body)
    copies[parts].wait()


def conv_kernel(idx_ref, first_ref, mid_ref, back_ref, last_ref, filt_ref, *refs, count):
    blocks, outs, (spot, mixed) = refs[:count], refs[count : 2 * count], refs[2 * count :]
    me = idx_ref[0]
    gather_positions(me, blocks, spot, count)
    forward_first(first_ref, spot, mixed)
    outer, _, inner, width = mixed.shape

    def middle(k):
        spec = jnp.dot(mid_ref[k], mixed[k].reshape(2 * inner, width), preferred_element_type=F32)
        filt = filt_ref[k].astype(F32)
        re, im = spec[:inner], spec[inner:]
        fre, fim = filt[:inner], filt[inner:]
        prod = jnp.concatenate([re * fre - im * fim, re * fim + im * fre], axis=0).astype(BF16)
        turned = jnp.dot(back_ref[k], prod, preferred_element_type=F32)
        mixed[k] = turned.astype(BF16).reshape(2, inner, width)

    for_each(outer, middle)

    def ending(i):
        rows = pl.ds(i * 2 * SUB, 2 * SUB)
        value = jnp.dot(last_ref[...], halves(mixed[:, :, rows, :]), preferred_element_type=F32)
        spot[:, rows, :] = joined(value, (outer,))

    for_each(inner // (2 * SUB), ending)
    here = outer // count
    for s in range(count):
        dst = lax.rem(me + s, count)
        outs[s][...] = spot[pl.ds(dst * here, here)].reshape(here * inner, width)


def hidden_rows(idx_ref, gain_ref, gate_ref, key_ref, value_ref, blocks, out_ref, at):
    me, count = idx_ref[0], len(blocks)
    width = blocks[0].shape[1]
    rows = slice(at, at + out_ref.shape[0])
    for s in range(count):
        src = lax.rem(me + count - s, count)
        cols = pl.ds(pl.multiple_of(src * width, width), width)
        gated = (key_ref[rows, cols].astype(F32) * value_ref[rows, cols].astype(F32)).astype(BF16).astype(F32)
        total = blocks[s][rows, :].astype(F32) + gain_ref[:, cols] * gated
        out_ref[:, cols] = (gate_ref[rows, cols].astype(F32) * total).astype(BF16)


def times_columns(hid_ref, weight_ref, part_ref, extra_ref=None):
    width = part_ref.shape[1]
    tile = min(256, width)
    for j in range(width // tile):
        cols = slice(j * tile, (j + 1) * tile)
        value = jnp.dot(hid_ref[...], weight_ref[:, cols], preferred_element_type=F32)
        if extra_ref is not None:
            value = value + extra_ref[:, cols].astype(F32)
        part_ref[:, cols] = value.astype(part_ref.dtype)


def rows_kernel(idx_ref, gain_ref, gate_ref, key_ref, value_ref, *refs, at, others, more):
    weights, refs = refs[:others], refs[others:]
    if more:
        own_ref, first_ref, *refs = refs
        *refs, own_first = refs
    *blocks, hid_ref, part_ref = refs
    if more:
        times_columns(first_ref, own_ref, own_first)
    hidden_rows(idx_ref, gain_ref, gate_ref, key_ref, value_ref, blocks, hid_ref, at)
    for j, weight_ref in enumerate(weights):
        cols = weight_ref.shape[1]
        times_columns(hid_ref, weight_ref, part_ref.at[:, j * cols : (j + 1) * cols])


def hidden_products(arrays, weights, blocks, at, rows, more=()):
    total, channels = arrays[2].shape
    columns = weights[0].shape[1]
    pinned = [pltpu.with_memory_space_constraint(w, pltpu.VMEM) for w in (*weights, *more)]
    limit = 2 * (len(pinned) + 1) * channels * columns + 12 * total * channels + 8 * total * columns
    outs = [pltpu.VMEM((rows, channels), BF16), pltpu.VMEM((rows, len(weights) * columns), BF16)]
    if more:
        outs.append(pltpu.VMEM((more[1].shape[0], columns), BF16))
    return pl.pallas_call(
        functools.partial(rows_kernel, at=at, others=len(weights), more=bool(more)),
        out_shape=outs,
        in_specs=[SMEM] + [VMEM] * (4 + len(pinned) + len(blocks)),
        out_specs=[VMEM] * len(outs),
        compiler_params=params(limit),
        cost_estimate=pl.CostEstimate(flops=4 * rows * channels * columns, bytes_accessed=limit, transcendentals=0),
    )(*arrays, *pinned, *blocks)


def own_kernel(hid_ref, weight_ref, crossed_ref, out_ref):
    times_columns(hid_ref, weight_ref, out_ref, crossed_ref.at[:, : out_ref.shape[1]])


def own_product(hidden, weight, crossed):
    rows, channels = hidden.shape
    columns = weight.shape[1]
    return pl.pallas_call(
        own_kernel,
        out_shape=pltpu.VMEM((rows, columns), BF16),
        in_specs=[VMEM] * 3,
        out_specs=VMEM,
        compiler_params=params(2 * channels * columns + 4 * rows * channels + 8 * rows * columns),
        cost_estimate=pl.CostEstimate(
            flops=2 * rows * channels * columns, bytes_accessed=2 * channels * columns, transcendentals=0
        ),
    )(*(pltpu.with_memory_space_constraint(a, pltpu.VMEM) for a in (hidden, weight, crossed)))


def late_kernel(group_ref, weight_ref, *refs, pieces, at):
    hids, extras = refs[:pieces], refs[pieces : 2 * pieces]
    parts, (held, sem) = refs[2 * pieces : -2], refs[-2:]
    width = held.shape[1]
    cols = pl.ds(pl.multiple_of(group_ref[0] * width, width), width)
    copy = pltpu.make_async_copy(weight_ref.at[:, cols], held, sem)
    copy.start()
    copy.wait()
    for r in range(pieces):
        times_columns(hids[r], held, parts[r], extras[r].at[:, at : at + width])


def late_product(group, hidden, weight, groups, extra, at, dtype):
    pieces = len(hidden)
    channels, width = weight.shape[0], weight.shape[1] // groups
    rows = sum(h.shape[0] for h in hidden)
    return pl.pallas_call(
        functools.partial(late_kernel, pieces=pieces, at=at),
        out_shape=[pltpu.VMEM((h.shape[0], width), dtype) for h in hidden],
        in_specs=[SMEM, HBM] + [VMEM] * (2 * pieces),
        out_specs=[VMEM] * pieces,
        scratch_shapes=[pltpu.VMEM((channels, width), BF16), pltpu.SemaphoreType.DMA],
        compiler_params=params(2 * channels * width + 2 * rows * channels + 2 * rows * weight.shape[1] + 6 * rows * width),
        cost_estimate=pl.CostEstimate(flops=0, bytes_accessed=channels, transcendentals=0),
    )(group, pltpu.with_memory_space_constraint(weight, pltpu.HBM), *hidden, *extra)


def add_kernel(own_ref, other_ref, out_ref):
    other = other_ref[:, : own_ref.shape[1]].astype(F32)
    out_ref[...] = (own_ref[...].astype(F32) + other).astype(BF16)


def add(own, other):
    return pl.pallas_call(
        add_kernel,
        out_shape=pltpu.VMEM(own.shape, BF16),
        in_specs=[VMEM] * 2,
        out_specs=VMEM,
        compiler_params=params(4 * own.size + 2 * other.size),
        cost_estimate=pl.CostEstimate(flops=own.size, bytes_accessed=6 * own.size, transcendentals=0),
    )(own, pltpu.with_memory_space_constraint(other, pltpu.VMEM))


def finish_kernel(*refs, at, terms):
    values, (out_ref, held, sem) = refs[:terms], refs[-3:]
    total = values[0][...]
    for value in values[1:]:
        total = total + value[...].astype(F32)
    held[...] = total.astype(BF16)
    rows = held.shape[0]
    copy = pltpu.make_async_copy(held, out_ref.at[pl.ds(at, rows), :], sem)
    copy.start()
    copy.wait()


def finish(values, at, rows, buffer):
    here, columns = values[0].shape
    aliased = [] if buffer is None else [buffer]
    return pl.pallas_call(
        functools.partial(finish_kernel, at=at, terms=len(values)),
        out_shape=jax.ShapeDtypeStruct((rows, columns), BF16),
        in_specs=[VMEM] * len(values) + [HBM] * len(aliased),
        out_specs=HBM,
        scratch_shapes=[pltpu.VMEM((here, columns), BF16), pltpu.SemaphoreType.DMA],
        input_output_aliases={len(values): 0} if aliased else {},
        compiler_params=params(4 * here * columns * (len(values) + 2)),
        cost_estimate=pl.CostEstimate(flops=0, bytes_accessed=columns, transcendentals=0),
    )(*(pltpu.with_memory_space_constraint(v, pltpu.VMEM) for v in values), *aliased)


def local(gate_q, key_k, value_v, long_filter, skip_gain, out_weight):
    rows, channels = key_k.shape
    count = lax.axis_size("ctx")
    groups = lax.axis_size("ch")
    chips = groups // 2
    total = rows * count
    inner = next(n for n in range(128, 0, -16) if rows % n == 0)
    outer = total // inner
    width = channels // count
    lanes = -(-width // 128) * 128
    idx = lax.axis_index("ctx").astype(jnp.int32).reshape(1)
    first, mid, back, last = tables(total, inner)
    spot = pltpu.VMEM((outer, inner, width), BF16)
    mixed = pltpu.VMEM((outer, 2, inner, width), BF16)
    signal = 2 * total * lanes
    table = 2 * (first.size + mid.size)

    here = lax.axis_index("ch").astype(jnp.int32)
    chip, core = here // 2, here % 2

    def group_of(step, which):
        return lax.rem(chip + step, chips) * 2 + which

    filter_in = exchange(filter_slices(idx, long_filter, count), "ctx", count)
    steps = list(range(1, chips)) + [0]
    order = jnp.stack([group_of(step, 1 - core) for step in steps] + [group_of(1, core)])
    slices, weights = gated_slices(idx, key_k, value_v, count, order, out_weight, groups)
    gated_in = exchange(slices, "ctx", count)
    spectrum, mid, back = pl.pallas_call(
        functools.partial(filter_kernel, count=count),
        out_shape=[
            jax.ShapeDtypeStruct((outer, 2 * inner, width), BF16),
            jax.ShapeDtypeStruct(mid.shape, BF16),
            jax.ShapeDtypeStruct(back.shape, BF16),
        ],
        in_specs=[SMEM, VMEM, HBM, HBM] + [VMEM] * count,
        out_specs=[VMEM] * 3,
        scratch_shapes=[spot, mixed, pltpu.SemaphoreType.DMA((5,))],
        compiler_params=params(2 * table + 6 * signal),
        cost_estimate=pl.CostEstimate(flops=3 * 10**9, bytes_accessed=8 * 10**6, transcendentals=0),
    )(
        idx,
        first,
        pltpu.with_memory_space_constraint(mid, pltpu.HBM),
        pltpu.with_memory_space_constraint(back, pltpu.HBM),
        *filter_in,
    )
    conv_out = pl.pallas_call(
        functools.partial(conv_kernel, count=count),
        out_shape=[jax.ShapeDtypeStruct((rows, width), BF16)] * count,
        in_specs=[SMEM] + [VMEM] * (5 + count),
        out_specs=[VMEM] * count,
        scratch_shapes=[spot, mixed],
        compiler_params=params(2 * table + 7 * signal),
        cost_estimate=pl.CostEstimate(flops=6 * 10**9, bytes_accessed=12 * 10**6, transcendentals=0),
    )(idx, first, mid, back, last, spectrum, *gated_in)
    conv_in = exchange(conv_out, "ctx", count)

    swap = [(i, i ^ 1) for i in range(groups)]
    lead = rows // 32 * 16

    def to_chip(part, step):
        return lax.ppermute(part, "ch", [(i, (i + 2 * step) % groups) for i in range(groups)])

    gain = skip_gain[None, :]
    if width % 128:
        conv = jnp.zeros((rows, channels), BF16)
        for s in range(count):
            src = lax.rem(idx[0] + count - s, count)
            conv = lax.dynamic_update_slice_in_dim(conv, conv_in[s], src * width, 1)
        idx, conv_in = jnp.zeros_like(idx), [conv]
    arrays = [idx, gain, gate_q, key_k, value_v]
    *others, own = weights
    hid_first, part_first = hidden_products(arrays, others, conv_in, 0, lead)
    crossed = [lax.ppermute(part_first, "ch", swap)]
    hid_rest, part_rest, sums = hidden_products(arrays, others, conv_in, lead, rows - lead, (own, hid_first))
    crossed.append(lax.ppermute(part_rest, "ch", swap))
    hidden = [hid_first, hid_rest]
    first_total = add(sums, crossed[0])
    arrived = [[to_chip(first_total, 1)], [to_chip(own_product(hid_rest, own, crossed[1]), 1)]]
    later = list(lax.optimization_barrier((*hidden, first_total))[:2])
    for j, step in enumerate(steps[1:-1]):
        totals = late_product(
            group_of(step, core).reshape(1), later, out_weight, groups, crossed, (j + 1) * own.shape[1], BF16
        )
        for got, total in zip(arrived, totals):
            got.append(to_chip(total, step))
    last_sums = late_product(
        group_of(0, core).reshape(1), later, out_weight, groups, crossed, (chips - 1) * own.shape[1], F32
    )
    first_rows = finish([last_sums[0]] + arrived[0], 0, rows, None)
    return finish([last_sums[1]] + arrived[1], lead, rows, first_rows)


def solution(mesh):
    placed = (
        P("ctx", "ch"),
        P("ctx", "ch"),
        P("ctx", "ch"),
        P("ctx", "ch"),
        P("ch"),
        P("ch", None),
    )
    return jax.shard_map(
        local, mesh=mesh, in_specs=placed, out_specs=P("ctx", "ch"), check_vma=False
    )
```

```python
import functools
import math

import jax
import jax.numpy as jnp
import numpy as np
from jax import lax
from jax.experimental import pallas as pl
from jax.experimental.pallas import tpu as pltpu
from jax.sharding import PartitionSpec as P

F32 = jnp.float32
BF16 = jnp.bfloat16
VMEM = pl.BlockSpec(memory_space=pltpu.VMEM)
SMEM = pl.BlockSpec(memory_space=pltpu.SMEM)
HBM = pl.BlockSpec(memory_space=pltpu.HBM)
SUB = 8


def params(nbytes):
    return pltpu.CompilerParams(vmem_limit_bytes=int(min(nbytes + 4 * 2**20, 58 * 2**20)))


def tables(total, inner):
    outer = total // inner
    n1 = np.arange(outer)
    eye = np.eye(SUB)
    ang = 2.0 * np.pi * np.outer(n1 + 0.25, n1) / outer
    first = np.stack([np.cos(ang), -np.sin(ang)], axis=1)
    first = np.einsum("kcn,ij->kcinj", first, eye).reshape(2 * outer * SUB, outer * SUB)
    last = np.stack([np.cos(ang), -np.sin(ang)], axis=1) / total
    last = np.einsum("kcn,ij->nikcj", last, eye).reshape(outer * SUB, 2 * outer * SUB)
    n2 = np.arange(inner)
    freq = n1[:, None] + outer * n2[None, :] + 0.25
    ang = 2.0 * np.pi * freq[:, :, None] * n2[None, None, :] / total
    cos, sin = np.cos(ang), np.sin(ang)
    mid = np.concatenate(
        [np.concatenate([cos, sin], axis=2), np.concatenate([-sin, cos], axis=2)], axis=1
    )
    back = np.swapaxes(mid, 1, 2)
    return tuple(jnp.asarray(np.ascontiguousarray(a).astype(jnp.bfloat16)) for a in (first, mid, back, last))


def split_kernel(idx_ref, array_ref, *outs, count):
    width = outs[0].shape[1]
    for s in range(count):
        at = pl.ds(pl.multiple_of(lax.rem(idx_ref[0] + s, count) * width, width), width)
        outs[s][...] = array_ref[:, at]


def filter_slices(idx, value, count):
    rows, channels = value.shape
    width = channels // count
    if width % 128:
        return [
            lax.dynamic_slice_in_dim(value, lax.rem(idx[0] + s, count) * width, width, 1)
            for s in range(count)
        ]
    return pl.pallas_call(
        functools.partial(split_kernel, count=count),
        out_shape=[jax.ShapeDtypeStruct((rows, width), BF16)] * count,
        in_specs=[SMEM, VMEM],
        out_specs=[VMEM] * count,
        compiler_params=params(4 * rows * channels),
        cost_estimate=pl.CostEstimate(flops=0, bytes_accessed=4 * rows * channels, transcendentals=0),
    )(idx, value)


def gate_kernel(idx_ref, order_ref, key_hbm, value_hbm, weight_ref, *refs, count):
    outs, columns = refs[:count], refs[count:-4]
    key_ref, value_ref, own_sems, sems = refs[-4:]
    width, cols = outs[0].shape[1], columns[0].shape[1]
    copies = [
        pltpu.make_async_copy(key_hbm, key_ref, own_sems.at[0]),
        pltpu.make_async_copy(value_hbm, value_ref, own_sems.at[1]),
    ]
    for j, column_ref in enumerate(columns):
        at = pl.ds(pl.multiple_of(order_ref[j] * cols, cols), cols)
        copies.append(pltpu.make_async_copy(weight_ref.at[:, at], column_ref, sems.at[j]))
    for copy in copies:
        copy.start()
    for copy in copies[:2]:
        copy.wait()
    for s in range(count):
        at = pl.ds(pl.multiple_of(lax.rem(idx_ref[0] + s, count) * width, width), width)
        outs[s][...] = (key_ref[:, at].astype(F32) * value_ref[:, at].astype(F32)).astype(BF16)
    for copy in copies[2:]:
        copy.wait()


def plain_kernel(order_ref, weight_ref, *refs):
    *columns, sems = refs
    cols = columns[0].shape[1]
    copies = []
    for j, column_ref in enumerate(columns):
        at = pl.ds(pl.multiple_of(order_ref[j] * cols, cols), cols)
        copies.append(pltpu.make_async_copy(weight_ref.at[:, at], column_ref, sems.at[j]))
        copies[-1].start()
    for copy in copies:
        copy.wait()


def gated_slices(idx, key_k, value_v, count, order, weight, groups):
    rows, channels = key_k.shape
    width, cols = channels // count, weight.shape[1] // groups
    picked = order.shape[0]
    weight = pltpu.with_memory_space_constraint(weight, pltpu.HBM)
    columns = [pltpu.VMEM((weight.shape[0], cols), BF16)] * picked
    limit = 8 * rows * channels + 2 * picked * weight.shape[0] * cols
    cost = pl.CostEstimate(flops=rows * channels, bytes_accessed=limit, transcendentals=0)
    if width % 128:
        gated = (key_k.astype(F32) * value_v.astype(F32)).astype(BF16)
        return filter_slices(idx, gated, count), pl.pallas_call(
            plain_kernel,
            out_shape=columns,
            in_specs=[SMEM, HBM],
            out_specs=[VMEM] * picked,
            scratch_shapes=[pltpu.SemaphoreType.DMA((picked,))],
            compiler_params=params(limit),
            cost_estimate=cost,
        )(order, weight)
    outs = pl.pallas_call(
        functools.partial(gate_kernel, count=count),
        out_shape=[jax.ShapeDtypeStruct((rows, width), BF16)] * count + columns,
        in_specs=[SMEM, SMEM] + [HBM] * 3,
        out_specs=[VMEM] * (count + picked),
        scratch_shapes=[pltpu.VMEM((rows, channels), BF16)] * 2
        + [pltpu.SemaphoreType.DMA((2,)), pltpu.SemaphoreType.DMA((picked,))],
        compiler_params=params(limit),
        cost_estimate=cost,
    )(
        idx,
        order,
        pltpu.with_memory_space_constraint(key_k, pltpu.HBM),
        pltpu.with_memory_space_constraint(value_v, pltpu.HBM),
        weight,
    )
    return outs[:count], outs[count:]


def exchange(blocks, axis, count):
    out = [blocks[0]]
    for s in range(1, count):
        out.append(lax.ppermute(blocks[s], axis, [(i, (i + s) % count) for i in range(count)]))
    return out


def gather_positions(me, blocks, spot, count):
    outer_here = blocks[0].shape[0] // spot.shape[1]
    for s in range(count):
        src = lax.rem(me + count - s, count)
        spot[pl.ds(src * outer_here, outer_here)] = blocks[s][...].reshape(outer_here, *spot.shape[1:])


def halves(tile):
    tile = tile.astype(F32)
    width = tile.shape[-1]
    return jnp.concatenate(
        [tile[..., at : at + SUB, :].reshape(-1, width).astype(BF16) for at in (0, SUB)], axis=1
    )


def joined(value, lead):
    width = value.shape[1] // 2
    parts = [value[:, at : at + width].reshape(*lead, SUB, width) for at in (0, width)]
    return jnp.concatenate(parts, axis=len(lead)).astype(BF16)


def for_each(count, body):
    if count <= 32:
        for i in range(count):
            body(i)
    else:
        lax.fori_loop(0, count, lambda i, c: (body(i), c)[1], 0, unroll=4 if count % 4 == 0 else 1)


def forward_first(first_ref, spot, mixed):
    outer, inner, _ = spot.shape

    def body(i):
        rows = pl.ds(i * 2 * SUB, 2 * SUB)
        value = jnp.dot(first_ref[...], halves(spot[:, rows, :]), preferred_element_type=F32)
        mixed[:, :, rows, :] = joined(value, (outer, 2))

    for_each(inner // (2 * SUB), body)


def filter_kernel(idx_ref, first_ref, mid_hbm, back_hbm, *refs, count):
    blocks, (out_ref, mid_ref, back_ref, spot, mixed, sems) = refs[:count], refs[count:]
    outer, _, inner, width = mixed.shape
    parts = sems.shape[0] - 1
    cuts = [outer * p // parts for p in range(parts + 1)]
    spans = [pl.ds(lo, hi - lo) for lo, hi in zip(cuts, cuts[1:])]
    copies = [pltpu.make_async_copy(mid_hbm.at[at], mid_ref.at[at], sems.at[p]) for p, at in enumerate(spans)]
    copies.append(pltpu.make_async_copy(back_hbm, back_ref, sems.at[parts]))
    for copy in copies:
        copy.start()
    gather_positions(idx_ref[0], blocks, spot, count)
    forward_first(first_ref, spot, mixed)

    for p in range(parts):
        copies[p].wait()

        def body(k):
            k = k + cuts[p]
            out_ref[k] = jnp.dot(
                mid_ref[k], mixed[k].reshape(2 * inner, width), preferred_element_type=F32
            ).astype(BF16)

        for_each(cuts[p + 1] - cuts[p], body)
    copies[parts].wait()


def conv_kernel(idx_ref, first_ref, mid_ref, back_ref, last_ref, filt_ref, *refs, count):
    blocks, outs, (spot, mixed) = refs[:count], refs[count : 2 * count], refs[2 * count :]
    me = idx_ref[0]
    gather_positions(me, blocks, spot, count)
    forward_first(first_ref, spot, mixed)
    outer, _, inner, width = mixed.shape

    def middle(k):
        spec = jnp.dot(mid_ref[k], mixed[k].reshape(2 * inner, width), preferred_element_type=F32)
        filt = filt_ref[k].astype(F32)
        re, im = spec[:inner], spec[inner:]
        fre, fim = filt[:inner], filt[inner:]
        prod = jnp.concatenate([re * fre - im * fim, re * fim + im * fre], axis=0).astype(BF16)
        turned = jnp.dot(back_ref[k], prod, preferred_element_type=F32)
        mixed[k] = turned.astype(BF16).reshape(2, inner, width)

    for_each(outer, middle)

    def ending(i):
        rows = pl.ds(i * 2 * SUB, 2 * SUB)
        value = jnp.dot(last_ref[...], halves(mixed[:, :, rows, :]), preferred_element_type=F32)
        spot[:, rows, :] = joined(value, (outer,))

    for_each(inner // (2 * SUB), ending)
    here = outer // count
    for s in range(count):
        dst = lax.rem(me + s, count)
        outs[s][...] = spot[pl.ds(dst * here, here)].reshape(here * inner, width)


def hidden_rows(idx_ref, gain_ref, gate_ref, key_ref, value_ref, blocks, out_ref, at):
    me, count = idx_ref[0], len(blocks)
    width = blocks[0].shape[1]
    rows = slice(at, at + out_ref.shape[0])
    for s in range(count):
        src = lax.rem(me + count - s, count)
        cols = pl.ds(pl.multiple_of(src * width, width), width)
        gated = (key_ref[rows, cols].astype(F32) * value_ref[rows, cols].astype(F32)).astype(BF16).astype(F32)
        total = blocks[s][rows, :].astype(F32) + gain_ref[:, cols] * gated
        out_ref[:, cols] = (gate_ref[rows, cols].astype(F32) * total).astype(BF16)


def times_columns(hid_ref, weight_ref, part_ref, extra_ref=None):
    width = part_ref.shape[1]
    tile = min(256, width)
    for j in range(width // tile):
        cols = slice(j * tile, (j + 1) * tile)
        value = jnp.dot(hid_ref[...], weight_ref[:, cols], preferred_element_type=F32)
        if extra_ref is not None:
            value = value + extra_ref[:, cols].astype(F32)
        part_ref[:, cols] = value.astype(part_ref.dtype)


def rows_kernel(idx_ref, gain_ref, gate_ref, key_ref, value_ref, *refs, at, others, more):
    weights, refs = refs[:others], refs[others:]
    if more:
        own_ref, first_ref, *refs = refs
        *refs, own_first = refs
    *blocks, hid_ref, part_ref = refs
    if more:
        times_columns(first_ref, own_ref, own_first)
    hidden_rows(idx_ref, gain_ref, gate_ref, key_ref, value_ref, blocks, hid_ref, at)
    for j, weight_ref in enumerate(weights):
        cols = weight_ref.shape[1]
        times_columns(hid_ref, weight_ref, part_ref.at[:, j * cols : (j + 1) * cols])


def hidden_products(arrays, weights, blocks, at, rows, more=()):
    total, channels = arrays[2].shape
    columns = weights[0].shape[1]
    pinned = [pltpu.with_memory_space_constraint(w, pltpu.VMEM) for w in (*weights, *more)]
    limit = 2 * (len(pinned) + 1) * channels * columns + 12 * total * channels + 8 * total * columns
    outs = [pltpu.VMEM((rows, channels), BF16), pltpu.VMEM((rows, len(weights) * columns), BF16)]
    if more:
        outs.append(pltpu.VMEM((more[1].shape[0], columns), BF16))
    return pl.pallas_call(
        functools.partial(rows_kernel, at=at, others=len(weights), more=bool(more)),
        out_shape=outs,
        in_specs=[SMEM] + [VMEM] * (4 + len(pinned) + len(blocks)),
        out_specs=[VMEM] * len(outs),
        compiler_params=params(limit),
        cost_estimate=pl.CostEstimate(flops=4 * rows * channels * columns, bytes_accessed=limit, transcendentals=0),
    )(*arrays, *pinned, *blocks)


def own_kernel(hid_ref, weight_ref, crossed_ref, out_ref, *, at):
    times_columns(hid_ref, weight_ref, out_ref, crossed_ref.at[:, at : at + out_ref.shape[1]])


def own_product(hidden, weight, crossed, at=0):
    rows, channels = hidden.shape
    columns = weight.shape[1]
    return pl.pallas_call(
        functools.partial(own_kernel, at=at),
        out_shape=pltpu.VMEM((rows, columns), BF16),
        in_specs=[VMEM] * 3,
        out_specs=VMEM,
        compiler_params=params(2 * channels * columns + 4 * rows * channels + 8 * rows * columns),
        cost_estimate=pl.CostEstimate(
            flops=2 * rows * channels * columns, bytes_accessed=2 * channels * columns, transcendentals=0
        ),
    )(*(pltpu.with_memory_space_constraint(a, pltpu.VMEM) for a in (hidden, weight, crossed)))


def add_kernel(own_ref, other_ref, out_ref):
    other = other_ref[:, : own_ref.shape[1]].astype(F32)
    out_ref[...] = (own_ref[...].astype(F32) + other).astype(BF16)


def add(own, other):
    return pl.pallas_call(
        add_kernel,
        out_shape=pltpu.VMEM(own.shape, BF16),
        in_specs=[VMEM] * 2,
        out_specs=VMEM,
        compiler_params=params(4 * own.size + 2 * other.size),
        cost_estimate=pl.CostEstimate(flops=own.size, bytes_accessed=6 * own.size, transcendentals=0),
    )(own, pltpu.with_memory_space_constraint(other, pltpu.VMEM))


def last_kernel(weight_ref, *refs, pieces, at):
    hids, extras, parts = refs[:pieces], refs[pieces : 2 * pieces], refs[2 * pieces :]
    for hid_ref, extra_ref, part_ref in zip(hids, extras, parts):
        times_columns(hid_ref, weight_ref, part_ref, extra_ref.at[:, at : at + part_ref.shape[1]])


def last_products(hidden, weight, crossed, at):
    channels, columns = weight.shape
    rows = sum(h.shape[0] for h in hidden)
    return pl.pallas_call(
        functools.partial(last_kernel, pieces=len(hidden), at=at),
        out_shape=[pltpu.VMEM((h.shape[0], columns), F32) for h in hidden],
        in_specs=[VMEM] * (1 + 2 * len(hidden)),
        out_specs=[VMEM] * len(hidden),
        compiler_params=params(2 * weight.size + 2 * rows * channels + 2 * sum(c.size for c in crossed) + 4 * rows * columns),
        cost_estimate=pl.CostEstimate(flops=0, bytes_accessed=channels, transcendentals=0),
    )(*(pltpu.with_memory_space_constraint(a, pltpu.VMEM) for a in (weight, *hidden, *crossed)))


def finish_kernel(*refs, at, terms):
    values, (out_ref, held, sem) = refs[:terms], refs[-3:]
    total = values[0][...]
    for value in values[1:]:
        total = total + value[...].astype(F32)
    held[...] = total.astype(BF16)
    rows = held.shape[0]
    copy = pltpu.make_async_copy(held, out_ref.at[pl.ds(at, rows), :], sem)
    copy.start()
    copy.wait()


def finish(values, at, rows, buffer):
    here, columns = values[0].shape
    aliased = [] if buffer is None else [buffer]
    return pl.pallas_call(
        functools.partial(finish_kernel, at=at, terms=len(values)),
        out_shape=jax.ShapeDtypeStruct((rows, columns), BF16),
        in_specs=[VMEM] * len(values) + [HBM] * len(aliased),
        out_specs=HBM,
        scratch_shapes=[pltpu.VMEM((here, columns), BF16), pltpu.SemaphoreType.DMA],
        input_output_aliases={len(values): 0} if aliased else {},
        compiler_params=params(4 * here * columns * (len(values) + 2)),
        cost_estimate=pl.CostEstimate(flops=0, bytes_accessed=columns, transcendentals=0),
    )(*(pltpu.with_memory_space_constraint(v, pltpu.VMEM) for v in values), *aliased)


def local(gate_q, key_k, value_v, long_filter, skip_gain, out_weight):
    rows, channels = key_k.shape
    count = lax.axis_size("ctx")
    groups = lax.axis_size("ch")
    chips = groups // 2
    total = rows * count
    inner = next(n for n in range(128, 0, -16) if rows % n == 0)
    outer = total // inner
    width = channels // count
    lanes = -(-width // 128) * 128
    idx = lax.axis_index("ctx").astype(jnp.int32).reshape(1)
    first, mid, back, last = tables(total, inner)
    spot = pltpu.VMEM((outer, inner, width), BF16)
    mixed = pltpu.VMEM((outer, 2, inner, width), BF16)
    signal = 2 * total * lanes
    table = 2 * (first.size + mid.size)

    here = lax.axis_index("ch").astype(jnp.int32)
    chip, core = here // 2, here % 2

    def group_of(step, which):
        return lax.rem(chip + step, chips) * 2 + which

    filter_in = exchange(filter_slices(idx, long_filter, count), "ctx", count)
    steps = list(range(1, chips)) + [0]
    order = jnp.stack([group_of(step, which) for which in (1 - core, core) for step in steps])
    slices, weights = gated_slices(idx, key_k, value_v, count, order, out_weight, groups)
    gated_in = exchange(slices, "ctx", count)
    spectrum, mid, back = pl.pallas_call(
        functools.partial(filter_kernel, count=count),
        out_shape=[
            jax.ShapeDtypeStruct((outer, 2 * inner, width), BF16),
            jax.ShapeDtypeStruct(mid.shape, BF16),
            jax.ShapeDtypeStruct(back.shape, BF16),
        ],
        in_specs=[SMEM, VMEM, HBM, HBM] + [VMEM] * count,
        out_specs=[VMEM] * 3,
        scratch_shapes=[spot, mixed, pltpu.SemaphoreType.DMA((5,))],
        compiler_params=params(2 * table + 6 * signal),
        cost_estimate=pl.CostEstimate(flops=3 * 10**9, bytes_accessed=8 * 10**6, transcendentals=0),
    )(
        idx,
        first,
        pltpu.with_memory_space_constraint(mid, pltpu.HBM),
        pltpu.with_memory_space_constraint(back, pltpu.HBM),
        *filter_in,
    )
    conv_out = pl.pallas_call(
        functools.partial(conv_kernel, count=count),
        out_shape=[jax.ShapeDtypeStruct((rows, width), BF16)] * count,
        in_specs=[SMEM] + [VMEM] * (5 + count),
        out_specs=[VMEM] * count,
        scratch_shapes=[spot, mixed],
        compiler_params=params(2 * table + 7 * signal),
        cost_estimate=pl.CostEstimate(flops=6 * 10**9, bytes_accessed=12 * 10**6, transcendentals=0),
    )(idx, first, mid, back, last, spectrum, *gated_in)
    conv_in = exchange(conv_out, "ctx", count)

    swap = [(i, i ^ 1) for i in range(groups)]
    lead = rows // 32 * 16

    def to_chip(part, step):
        return lax.ppermute(part, "ch", [(i, (i + 2 * step) % groups) for i in range(groups)])

    gain = skip_gain[None, :]
    if width % 128:
        conv = jnp.zeros((rows, channels), BF16)
        for s in range(count):
            src = lax.rem(idx[0] + count - s, count)
            conv = lax.dynamic_update_slice_in_dim(conv, conv_in[s], src * width, 1)
        idx, conv_in = jnp.zeros_like(idx), [conv]
    arrays = [idx, gain, gate_q, key_k, value_v]
    others, owns = weights[:chips], weights[chips:]
    columns = owns[0].shape[1]
    hid_first, part_first = hidden_products(arrays, others, conv_in, 0, lead)
    crossed = [lax.ppermute(part_first, "ch", swap)]
    hid_rest, part_rest, sums = hidden_products(arrays, others, conv_in, lead, rows - lead, (owns[0], hid_first))
    crossed.append(lax.ppermute(part_rest, "ch", swap))
    arrived = [[to_chip(add(sums, crossed[0]), 1)], [to_chip(own_product(hid_rest, owns[0], crossed[1]), 1)]]
    for j, step in enumerate(steps[1:-1]):
        for got, hid, cross in zip(arrived, (hid_first, hid_rest), crossed):
            got.append(to_chip(own_product(hid, owns[j + 1], cross, (j + 1) * columns), step))
    last = (chips - 1) * columns
    sums = last_products((hid_first, hid_rest), owns[-1], crossed, last)
    out = finish([sums[0]] + arrived[0], 0, rows, None)
    return finish([sums[1]] + arrived[1], lead, rows, out)


def solution(mesh):
    placed = (
        P("ctx", "ch"),
        P("ctx", "ch"),
        P("ctx", "ch"),
        P("ctx", "ch"),
        P("ch"),
        P("ch", None),
    )
    return jax.shard_map(
        local, mesh=mesh, in_specs=placed, out_specs=P("ctx", "ch"), check_vma=False
    )
```

```python
import functools
import math

import jax
import jax.numpy as jnp
import numpy as np
from jax import lax
from jax.experimental import pallas as pl
from jax.experimental.pallas import tpu as pltpu
from jax.sharding import PartitionSpec as P

F32 = jnp.float32
BF16 = jnp.bfloat16
VMEM = pl.BlockSpec(memory_space=pltpu.VMEM)
SMEM = pl.BlockSpec(memory_space=pltpu.SMEM)
HBM = pl.BlockSpec(memory_space=pltpu.HBM)
SUB = 8


def params(nbytes):
    return pltpu.CompilerParams(vmem_limit_bytes=int(min(nbytes + 4 * 2**20, 58 * 2**20)))


def filter_order(count):
    return list(range(count))


def gated_order(count):
    return list(range(count))


def conv_order(count):
    if count < 4:
        return list(range(count))
    return [0, count // 2, 1, count - 1, *sorted(set(range(2, count - 1)) - {count // 2}, key=lambda s: (abs(2 * s - count), s))]


def tables(total, inner):
    outer = total // inner
    n1 = np.arange(outer)
    eye = np.eye(SUB)
    ang = 2.0 * np.pi * np.outer(n1 + 0.25, n1) / outer
    first = np.stack([np.cos(ang), -np.sin(ang)], axis=1)
    first = np.einsum("kcn,ij->kcinj", first, eye).reshape(2 * outer * SUB, outer * SUB)
    last = np.stack([np.cos(ang), -np.sin(ang)], axis=1) / total
    last = np.einsum("kcn,ij->nikcj", last, eye).reshape(outer * SUB, 2 * outer * SUB)
    n2 = np.arange(inner)
    freq = n1[:, None] + outer * n2[None, :] + 0.25
    ang = 2.0 * np.pi * freq[:, :, None] * n2[None, None, :] / total
    cos, sin = np.cos(ang), np.sin(ang)
    mid = np.concatenate(
        [np.concatenate([cos, sin], axis=2), np.concatenate([-sin, cos], axis=2)], axis=1
    )
    back = np.swapaxes(mid, 1, 2)
    return tuple(jnp.asarray(np.ascontiguousarray(a).astype(jnp.bfloat16)) for a in (first, mid, back, last))


def split_kernel(idx_ref, array_ref, *outs, count):
    width = outs[0].shape[1]
    for j, s in enumerate(filter_order(count)):
        at = pl.ds(pl.multiple_of(lax.rem(idx_ref[0] + s, count) * width, width), width)
        outs[j][...] = array_ref[:, at]


def filter_slices(idx, value, count, order):
    rows, channels = value.shape
    width = channels // count
    if width % 128:
        return [
            lax.dynamic_slice_in_dim(value, lax.rem(idx[0] + s, count) * width, width, 1)
            for s in order(count)
        ]
    return pl.pallas_call(
        functools.partial(split_kernel, count=count),
        out_shape=[jax.ShapeDtypeStruct((rows, width), BF16)] * count,
        in_specs=[SMEM, VMEM],
        out_specs=[VMEM] * count,
        compiler_params=params(4 * rows * channels),
        cost_estimate=pl.CostEstimate(flops=0, bytes_accessed=4 * rows * channels, transcendentals=0),
    )(idx, value)


def gate_kernel(idx_ref, order_ref, key_hbm, value_hbm, weight_ref, *refs, count):
    outs, columns = refs[:count], refs[count:-4]
    key_ref, value_ref, own_sems, sems = refs[-4:]
    width, cols = outs[0].shape[1], columns[0].shape[1]
    copies = [
        pltpu.make_async_copy(key_hbm, key_ref, own_sems.at[0]),
        pltpu.make_async_copy(value_hbm, value_ref, own_sems.at[1]),
    ]
    for j, column_ref in enumerate(columns):
        at = pl.ds(pl.multiple_of(order_ref[j] * cols, cols), cols)
        copies.append(pltpu.make_async_copy(weight_ref.at[:, at], column_ref, sems.at[j]))
    for copy in copies:
        copy.start()
    for copy in copies[:2]:
        copy.wait()
    for j, s in enumerate(gated_order(count)):
        at = pl.ds(pl.multiple_of(lax.rem(idx_ref[0] + s, count) * width, width), width)
        outs[j][...] = (key_ref[:, at].astype(F32) * value_ref[:, at].astype(F32)).astype(BF16)
    for copy in copies[2:]:
        copy.wait()


def plain_kernel(order_ref, weight_ref, *refs):
    *columns, sems = refs
    cols = columns[0].shape[1]
    copies = []
    for j, column_ref in enumerate(columns):
        at = pl.ds(pl.multiple_of(order_ref[j] * cols, cols), cols)
        copies.append(pltpu.make_async_copy(weight_ref.at[:, at], column_ref, sems.at[j]))
        copies[-1].start()
    for copy in copies:
        copy.wait()


def gated_slices(idx, key_k, value_v, count, order, weight, groups):
    rows, channels = key_k.shape
    width, cols = channels // count, weight.shape[1] // groups
    picked = order.shape[0]
    weight = pltpu.with_memory_space_constraint(weight, pltpu.HBM)
    columns = [pltpu.VMEM((weight.shape[0], cols), BF16)] * picked
    limit = 8 * rows * channels + 2 * picked * weight.shape[0] * cols
    cost = pl.CostEstimate(flops=rows * channels, bytes_accessed=limit, transcendentals=0)
    if width % 128:
        gated = (key_k.astype(F32) * value_v.astype(F32)).astype(BF16)
        return filter_slices(idx, gated, count, gated_order), pl.pallas_call(
            plain_kernel,
            out_shape=columns,
            in_specs=[SMEM, HBM],
            out_specs=[VMEM] * picked,
            scratch_shapes=[pltpu.SemaphoreType.DMA((picked,))],
            compiler_params=params(limit),
            cost_estimate=cost,
        )(order, weight)
    outs = pl.pallas_call(
        functools.partial(gate_kernel, count=count),
        out_shape=[jax.ShapeDtypeStruct((rows, width), BF16)] * count + columns,
        in_specs=[SMEM, SMEM] + [HBM] * 3,
        out_specs=[VMEM] * (count + picked),
        scratch_shapes=[pltpu.VMEM((rows, channels), BF16)] * 2
        + [pltpu.SemaphoreType.DMA((2,)), pltpu.SemaphoreType.DMA((picked,))],
        compiler_params=params(limit),
        cost_estimate=cost,
    )(
        idx,
        order,
        pltpu.with_memory_space_constraint(key_k, pltpu.HBM),
        pltpu.with_memory_space_constraint(value_v, pltpu.HBM),
        weight,
    )
    return outs[:count], outs[count:]


def exchange(blocks, axis, order):
    count = len(blocks)
    out = []
    for s, block in zip(order, blocks):
        perm = [(i, (i + s) % count) for i in range(count)]
        out.append(lax.ppermute(block, axis, perm) if s else block)
    return out


def gather_positions(me, blocks, spot, count, order):
    outer_here = blocks[0].shape[0] // spot.shape[1]
    for j, s in enumerate(order(count)):
        src = lax.rem(me + count - s, count)
        spot[pl.ds(src * outer_here, outer_here)] = blocks[j][...].reshape(outer_here, *spot.shape[1:])


def halves(tile):
    tile = tile.astype(F32)
    width = tile.shape[-1]
    return jnp.concatenate(
        [tile[..., at : at + SUB, :].reshape(-1, width).astype(BF16) for at in (0, SUB)], axis=1
    )


def joined(value, lead):
    width = value.shape[1] // 2
    parts = [value[:, at : at + width].reshape(*lead, SUB, width) for at in (0, width)]
    return jnp.concatenate(parts, axis=len(lead)).astype(BF16)


def for_each(count, body):
    if count <= 32:
        for i in range(count):
            body(i)
    else:
        lax.fori_loop(0, count, lambda i, c: (body(i), c)[1], 0, unroll=4 if count % 4 == 0 else 1)


def forward_first(first_ref, spot, mixed):
    outer, inner, _ = spot.shape

    def body(i):
        rows = pl.ds(i * 2 * SUB, 2 * SUB)
        value = jnp.dot(first_ref[...], halves(spot[:, rows, :]), preferred_element_type=F32)
        mixed[:, :, rows, :] = joined(value, (outer, 2))

    for_each(inner // (2 * SUB), body)


def filter_kernel(idx_ref, first_ref, mid_hbm, back_hbm, *refs, count):
    blocks, (out_ref, mid_ref, back_ref, spot, mixed, sems) = refs[:count], refs[count:]
    outer, _, inner, width = mixed.shape
    parts = sems.shape[0] - 1
    cuts = [outer * p // parts for p in range(parts + 1)]
    spans = [pl.ds(lo, hi - lo) for lo, hi in zip(cuts, cuts[1:])]
    copies = [pltpu.make_async_copy(mid_hbm.at[at], mid_ref.at[at], sems.at[p]) for p, at in enumerate(spans)]
    copies.append(pltpu.make_async_copy(back_hbm, back_ref, sems.at[parts]))
    for copy in copies:
        copy.start()
    gather_positions(idx_ref[0], blocks, spot, count, filter_order)
    forward_first(first_ref, spot, mixed)

    for p in range(parts):
        copies[p].wait()

        def body(k):
            k = k + cuts[p]
            out_ref[k] = jnp.dot(
                mid_ref[k], mixed[k].reshape(2 * inner, width), preferred_element_type=F32
            ).astype(BF16)

        for_each(cuts[p + 1] - cuts[p], body)
    copies[parts].wait()


def conv_kernel(idx_ref, first_ref, mid_ref, back_ref, last_ref, filt_ref, *refs, count):
    blocks, outs, (spot, mixed) = refs[:count], refs[count : 2 * count], refs[2 * count :]
    me = idx_ref[0]
    gather_positions(me, blocks, spot, count, gated_order)
    forward_first(first_ref, spot, mixed)
    outer, _, inner, width = mixed.shape

    def middle(k):
        spec = jnp.dot(mid_ref[k], mixed[k].reshape(2 * inner, width), preferred_element_type=F32)
        filt = filt_ref[k].astype(F32)
        re, im = spec[:inner], spec[inner:]
        fre, fim = filt[:inner], filt[inner:]
        prod = jnp.concatenate([re * fre - im * fim, re * fim + im * fre], axis=0).astype(BF16)
        turned = jnp.dot(back_ref[k], prod, preferred_element_type=F32)
        mixed[k] = turned.astype(BF16).reshape(2, inner, width)

    for_each(outer, middle)

    def ending(i):
        rows = pl.ds(i * 2 * SUB, 2 * SUB)
        value = jnp.dot(last_ref[...], halves(mixed[:, :, rows, :]), preferred_element_type=F32)
        spot[:, rows, :] = joined(value, (outer,))

    for_each(inner // (2 * SUB), ending)
    here = outer // count
    for j, s in enumerate(conv_order(count)):
        dst = lax.rem(me + s, count)
        outs[j][...] = spot[pl.ds(dst * here, here)].reshape(here * inner, width)


def hidden_rows(idx_ref, gain_ref, gate_ref, key_ref, value_ref, blocks, out_ref, at):
    me, count = idx_ref[0], len(blocks)
    width = blocks[0].shape[1]
    rows = slice(at, at + out_ref.shape[0])
    for j, s in enumerate(conv_order(count)):
        src = lax.rem(me + count - s, count)
        cols = pl.ds(pl.multiple_of(src * width, width), width)
        gated = (key_ref[rows, cols].astype(F32) * value_ref[rows, cols].astype(F32)).astype(BF16).astype(F32)
        total = blocks[j][rows, :].astype(F32) + gain_ref[:, cols] * gated
        out_ref[:, cols] = (gate_ref[rows, cols].astype(F32) * total).astype(BF16)


def times_columns(hid_ref, weight_ref, part_ref, extra_ref=None):
    width = part_ref.shape[1]
    tile = min(256, width)
    for j in range(width // tile):
        cols = slice(j * tile, (j + 1) * tile)
        value = jnp.dot(hid_ref[...], weight_ref[:, cols], preferred_element_type=F32)
        if extra_ref is not None:
            value = value + extra_ref[:, cols].astype(F32)
        part_ref[:, cols] = value.astype(part_ref.dtype)


def rows_kernel(idx_ref, gain_ref, gate_ref, key_ref, value_ref, *refs, at, others, more):
    weights, refs = refs[:others], refs[others:]
    if more:
        own_ref, first_ref, *refs = refs
        *refs, own_first = refs
    *blocks, hid_ref, part_ref = refs
    if more:
        times_columns(first_ref, own_ref, own_first)
    hidden_rows(idx_ref, gain_ref, gate_ref, key_ref, value_ref, blocks, hid_ref, at)
    for j, weight_ref in enumerate(weights):
        cols = weight_ref.shape[1]
        times_columns(hid_ref, weight_ref, part_ref.at[:, j * cols : (j + 1) * cols])


def hidden_products(arrays, weights, blocks, at, rows, more=()):
    total, channels = arrays[2].shape
    columns = weights[0].shape[1]
    pinned = [pltpu.with_memory_space_constraint(w, pltpu.VMEM) for w in (*weights, *more)]
    limit = 2 * (len(pinned) + 1) * channels * columns + 12 * total * channels + 8 * total * columns
    outs = [pltpu.VMEM((rows, channels), BF16), pltpu.VMEM((rows, len(weights) * columns), BF16)]
    if more:
        outs.append(pltpu.VMEM((more[1].shape[0], columns), BF16))
    return pl.pallas_call(
        functools.partial(rows_kernel, at=at, others=len(weights), more=bool(more)),
        out_shape=outs,
        in_specs=[SMEM] + [VMEM] * (4 + len(pinned) + len(blocks)),
        out_specs=[VMEM] * len(outs),
        compiler_params=params(limit),
        cost_estimate=pl.CostEstimate(flops=4 * rows * channels * columns, bytes_accessed=limit, transcendentals=0),
    )(*arrays, *pinned, *blocks)


def own_kernel(hid_ref, weight_ref, crossed_ref, out_ref, *, at):
    times_columns(hid_ref, weight_ref, out_ref, crossed_ref.at[:, at : at + out_ref.shape[1]])


def own_product(hidden, weight, crossed, at=0):
    rows, channels = hidden.shape
    columns = weight.shape[1]
    return pl.pallas_call(
        functools.partial(own_kernel, at=at),
        out_shape=pltpu.VMEM((rows, columns), BF16),
        in_specs=[VMEM] * 3,
        out_specs=VMEM,
        compiler_params=params(2 * channels * columns + 4 * rows * channels + 8 * rows * columns),
        cost_estimate=pl.CostEstimate(
            flops=2 * rows * channels * columns, bytes_accessed=2 * channels * columns, transcendentals=0
        ),
    )(*(pltpu.with_memory_space_constraint(a, pltpu.VMEM) for a in (hidden, weight, crossed)))


def add_kernel(own_ref, other_ref, out_ref):
    other = other_ref[:, : own_ref.shape[1]].astype(F32)
    out_ref[...] = (own_ref[...].astype(F32) + other).astype(BF16)


def add(own, other):
    return pl.pallas_call(
        add_kernel,
        out_shape=pltpu.VMEM(own.shape, BF16),
        in_specs=[VMEM] * 2,
        out_specs=VMEM,
        compiler_params=params(4 * own.size + 2 * other.size),
        cost_estimate=pl.CostEstimate(flops=own.size, bytes_accessed=6 * own.size, transcendentals=0),
    )(own, pltpu.with_memory_space_constraint(other, pltpu.VMEM))


def last_kernel(weight_ref, *refs, pieces, at):
    hids, extras, parts = refs[:pieces], refs[pieces : 2 * pieces], refs[2 * pieces :]
    for hid_ref, extra_ref, part_ref in zip(hids, extras, parts):
        times_columns(hid_ref, weight_ref, part_ref, extra_ref.at[:, at : at + part_ref.shape[1]])


def last_products(hidden, weight, crossed, at):
    channels, columns = weight.shape
    rows = sum(h.shape[0] for h in hidden)
    return pl.pallas_call(
        functools.partial(last_kernel, pieces=len(hidden), at=at),
        out_shape=[pltpu.VMEM((h.shape[0], columns), F32) for h in hidden],
        in_specs=[VMEM] * (1 + 2 * len(hidden)),
        out_specs=[VMEM] * len(hidden),
        compiler_params=params(2 * weight.size + 2 * rows * channels + 2 * sum(c.size for c in crossed) + 4 * rows * columns),
        cost_estimate=pl.CostEstimate(flops=0, bytes_accessed=channels, transcendentals=0),
    )(*(pltpu.with_memory_space_constraint(a, pltpu.VMEM) for a in (weight, *hidden, *crossed)))


def finish_kernel(*refs, at, terms):
    values, (out_ref, held, sem) = refs[:terms], refs[-3:]
    total = values[0][...]
    for value in values[1:]:
        total = total + value[...].astype(F32)
    held[...] = total.astype(BF16)
    rows = held.shape[0]
    copy = pltpu.make_async_copy(held, out_ref.at[pl.ds(at, rows), :], sem)
    copy.start()
    copy.wait()


def finish(values, at, rows, buffer):
    here, columns = values[0].shape
    aliased = [] if buffer is None else [buffer]
    return pl.pallas_call(
        functools.partial(finish_kernel, at=at, terms=len(values)),
        out_shape=jax.ShapeDtypeStruct((rows, columns), BF16),
        in_specs=[VMEM] * len(values) + [HBM] * len(aliased),
        out_specs=HBM,
        scratch_shapes=[pltpu.VMEM((here, columns), BF16), pltpu.SemaphoreType.DMA],
        input_output_aliases={len(values): 0} if aliased else {},
        compiler_params=params(4 * here * columns * (len(values) + 2)),
        cost_estimate=pl.CostEstimate(flops=0, bytes_accessed=columns, transcendentals=0),
    )(*(pltpu.with_memory_space_constraint(v, pltpu.VMEM) for v in values), *aliased)


def local(gate_q, key_k, value_v, long_filter, skip_gain, out_weight):
    rows, channels = key_k.shape
    count = lax.axis_size("ctx")
    groups = lax.axis_size("ch")
    chips = groups // 2
    total = rows * count
    inner = next(n for n in range(128, 0, -16) if rows % n == 0)
    outer = total // inner
    width = channels // count
    lanes = -(-width // 128) * 128
    idx = lax.axis_index("ctx").astype(jnp.int32).reshape(1)
    first, mid, back, last = tables(total, inner)
    spot = pltpu.VMEM((outer, inner, width), BF16)
    mixed = pltpu.VMEM((outer, 2, inner, width), BF16)
    signal = 2 * total * lanes
    table = 2 * (first.size + mid.size)

    here = lax.axis_index("ch").astype(jnp.int32)
    chip, core = here // 2, here % 2

    def group_of(step, which):
        return lax.rem(chip + step, chips) * 2 + which

    filter_in = exchange(filter_slices(idx, long_filter, count, filter_order), "ctx", filter_order(count))
    steps = list(range(1, chips)) + [0]
    order = jnp.stack([group_of(step, which) for which in (1 - core, core) for step in steps])
    slices, weights = gated_slices(idx, key_k, value_v, count, order, out_weight, groups)
    gated_in = exchange(slices, "ctx", gated_order(count))
    spectrum, mid, back = pl.pallas_call(
        functools.partial(filter_kernel, count=count),
        out_shape=[
            jax.ShapeDtypeStruct((outer, 2 * inner, width), BF16),
            jax.ShapeDtypeStruct(mid.shape, BF16),
            jax.ShapeDtypeStruct(back.shape, BF16),
        ],
        in_specs=[SMEM, VMEM, HBM, HBM] + [VMEM] * count,
        out_specs=[VMEM] * 3,
        scratch_shapes=[spot, mixed, pltpu.SemaphoreType.DMA((5,))],
        compiler_params=params(2 * table + 6 * signal),
        cost_estimate=pl.CostEstimate(flops=3 * 10**9, bytes_accessed=8 * 10**6, transcendentals=0),
    )(
        idx,
        first,
        pltpu.with_memory_space_constraint(mid, pltpu.HBM),
        pltpu.with_memory_space_constraint(back, pltpu.HBM),
        *filter_in,
    )
    conv_out = pl.pallas_call(
        functools.partial(conv_kernel, count=count),
        out_shape=[jax.ShapeDtypeStruct((rows, width), BF16)] * count,
        in_specs=[SMEM] + [VMEM] * (5 + count),
        out_specs=[VMEM] * count,
        scratch_shapes=[spot, mixed],
        compiler_params=params(2 * table + 7 * signal),
        cost_estimate=pl.CostEstimate(flops=6 * 10**9, bytes_accessed=12 * 10**6, transcendentals=0),
    )(idx, first, mid, back, last, spectrum, *gated_in)
    conv_in = exchange(conv_out, "ctx", conv_order(count))

    swap = [(i, i ^ 1) for i in range(groups)]
    lead = rows // 32 * 16

    def to_chip(part, step):
        return lax.ppermute(part, "ch", [(i, (i + 2 * step) % groups) for i in range(groups)])

    gain = skip_gain[None, :]
    if width % 128:
        conv = jnp.zeros((rows, channels), BF16)
        for j, s in enumerate(conv_order(count)):
            src = lax.rem(idx[0] + count - s, count)
            conv = lax.dynamic_update_slice_in_dim(conv, conv_in[j], src * width, 1)
        idx, conv_in = jnp.zeros_like(idx), [conv]
    arrays = [idx, gain, gate_q, key_k, value_v]
    others, owns = weights[:chips], weights[chips:]
    columns = owns[0].shape[1]
    hid_first, part_first = hidden_products(arrays, others, conv_in, 0, lead)
    crossed = [lax.ppermute(part_first, "ch", swap)]
    hid_rest, part_rest, sums = hidden_products(arrays, others, conv_in, lead, rows - lead, (owns[0], hid_first))
    crossed.append(lax.ppermute(part_rest, "ch", swap))
    arrived = [[to_chip(add(sums, crossed[0]), 1)], [to_chip(own_product(hid_rest, owns[0], crossed[1]), 1)]]
    for j, step in enumerate(steps[1:-1]):
        for got, hid, cross in zip(arrived, (hid_first, hid_rest), crossed):
            got.append(to_chip(own_product(hid, owns[j + 1], cross, (j + 1) * columns), step))
    last = (chips - 1) * columns
    sums = last_products((hid_first, hid_rest), owns[-1], crossed, last)
    out = finish([sums[0]] + arrived[0], 0, rows, None)
    return finish([sums[1]] + arrived[1], lead, rows, out)


def solution(mesh):
    placed = (
        P("ctx", "ch"),
        P("ctx", "ch"),
        P("ctx", "ch"),
        P("ctx", "ch"),
        P("ch"),
        P("ch", None),
    )
    return jax.shard_map(
        local, mesh=mesh, in_specs=placed, out_specs=P("ctx", "ch"), check_vma=False
    )
```

```python
import functools
import math

import jax
import jax.numpy as jnp
import numpy as np
from jax import lax
from jax.experimental import pallas as pl
from jax.experimental.pallas import tpu as pltpu
from jax.sharding import PartitionSpec as P

F32 = jnp.float32
BF16 = jnp.bfloat16
VMEM = pl.BlockSpec(memory_space=pltpu.VMEM)
SMEM = pl.BlockSpec(memory_space=pltpu.SMEM)
HBM = pl.BlockSpec(memory_space=pltpu.HBM)
SUB = 8


def params(nbytes):
    return pltpu.CompilerParams(vmem_limit_bytes=int(min(nbytes + 4 * 2**20, 58 * 2**20)))


def filter_order(count):
    return list(range(count))


def gated_order(count):
    return list(range(count))


def conv_order(count):
    if count < 4:
        return list(range(count))
    return [0, count // 2, 1, count - 1, *sorted(set(range(2, count - 1)) - {count // 2}, key=lambda s: (abs(2 * s - count), s))]


def tables(total, inner):
    outer = total // inner
    n1 = np.arange(outer)
    eye = np.eye(SUB)
    ang = 2.0 * np.pi * np.outer(n1 + 0.25, n1) / outer
    first = np.stack([np.cos(ang), -np.sin(ang)], axis=1)
    first = np.einsum("kcn,ij->kcinj", first, eye).reshape(2 * outer * SUB, outer * SUB)
    last = np.stack([np.cos(ang), -np.sin(ang)], axis=1) / total
    last = np.einsum("kcn,ij->nikcj", last, eye).reshape(outer * SUB, 2 * outer * SUB)
    n2 = np.arange(inner)
    freq = n1[:, None] + outer * n2[None, :] + 0.25
    ang = 2.0 * np.pi * freq[:, :, None] * n2[None, None, :] / total
    cos, sin = np.cos(ang), np.sin(ang)
    mid = np.concatenate(
        [np.concatenate([cos, sin], axis=2), np.concatenate([-sin, cos], axis=2)], axis=1
    )
    back = np.swapaxes(mid, 1, 2)
    return tuple(jnp.asarray(np.ascontiguousarray(a).astype(jnp.bfloat16)) for a in (first, mid, back, last))


def split_kernel(idx_ref, array_ref, *outs, count):
    width = outs[0].shape[1]
    for j, s in enumerate(filter_order(count)):
        at = pl.ds(pl.multiple_of(lax.rem(idx_ref[0] + s, count) * width, width), width)
        outs[j][...] = array_ref[:, at]


def filter_slices(idx, value, count, order):
    rows, channels = value.shape
    width = channels // count
    if width % 128:
        return [
            lax.dynamic_slice_in_dim(value, lax.rem(idx[0] + s, count) * width, width, 1)
            for s in order(count)
        ]
    return pl.pallas_call(
        functools.partial(split_kernel, count=count),
        out_shape=[jax.ShapeDtypeStruct((rows, width), BF16)] * count,
        in_specs=[SMEM, VMEM],
        out_specs=[VMEM] * count,
        compiler_params=params(4 * rows * channels),
        cost_estimate=pl.CostEstimate(flops=0, bytes_accessed=4 * rows * channels, transcendentals=0),
    )(idx, value)


def gate_kernel(idx_ref, order_ref, key_hbm, value_hbm, weight_ref, *refs, count):
    outs, columns = refs[:count], refs[count:-4]
    key_ref, value_ref, own_sems, sems = refs[-4:]
    width, cols = outs[0].shape[1], columns[0].shape[1]
    copies = [
        pltpu.make_async_copy(key_hbm, key_ref, own_sems.at[0]),
        pltpu.make_async_copy(value_hbm, value_ref, own_sems.at[1]),
    ]
    for j, column_ref in enumerate(columns):
        at = pl.ds(pl.multiple_of(order_ref[j] * cols, cols), cols)
        copies.append(pltpu.make_async_copy(weight_ref.at[:, at], column_ref, sems.at[j]))
    for copy in copies:
        copy.start()
    for copy in copies[:2]:
        copy.wait()
    for j, s in enumerate(gated_order(count)):
        at = pl.ds(pl.multiple_of(lax.rem(idx_ref[0] + s, count) * width, width), width)
        outs[j][...] = (key_ref[:, at].astype(F32) * value_ref[:, at].astype(F32)).astype(BF16)
    for copy in copies[2:]:
        copy.wait()


def plain_kernel(order_ref, weight_ref, *refs):
    *columns, sems = refs
    cols = columns[0].shape[1]
    copies = []
    for j, column_ref in enumerate(columns):
        at = pl.ds(pl.multiple_of(order_ref[j] * cols, cols), cols)
        copies.append(pltpu.make_async_copy(weight_ref.at[:, at], column_ref, sems.at[j]))
        copies[-1].start()
    for copy in copies:
        copy.wait()


def gated_slices(idx, key_k, value_v, count, order, weight, groups):
    rows, channels = key_k.shape
    width, cols = channels // count, weight.shape[1] // groups
    picked = order.shape[0]
    weight = pltpu.with_memory_space_constraint(weight, pltpu.HBM)
    columns = [pltpu.VMEM((weight.shape[0], cols), BF16)] * picked
    limit = 8 * rows * channels + 2 * picked * weight.shape[0] * cols
    cost = pl.CostEstimate(flops=rows * channels, bytes_accessed=limit, transcendentals=0)
    if width % 128:
        gated = (key_k.astype(F32) * value_v.astype(F32)).astype(BF16)
        return filter_slices(idx, gated, count, gated_order), pl.pallas_call(
            plain_kernel,
            out_shape=columns,
            in_specs=[SMEM, HBM],
            out_specs=[VMEM] * picked,
            scratch_shapes=[pltpu.SemaphoreType.DMA((picked,))],
            compiler_params=params(limit),
            cost_estimate=cost,
        )(order, weight)
    outs = pl.pallas_call(
        functools.partial(gate_kernel, count=count),
        out_shape=[jax.ShapeDtypeStruct((rows, width), BF16)] * count + columns,
        in_specs=[SMEM, SMEM] + [HBM] * 3,
        out_specs=[VMEM] * (count + picked),
        scratch_shapes=[pltpu.VMEM((rows, channels), BF16)] * 2
        + [pltpu.SemaphoreType.DMA((2,)), pltpu.SemaphoreType.DMA((picked,))],
        compiler_params=params(limit),
        cost_estimate=cost,
    )(
        idx,
        order,
        pltpu.with_memory_space_constraint(key_k, pltpu.HBM),
        pltpu.with_memory_space_constraint(value_v, pltpu.HBM),
        weight,
    )
    return outs[:count], outs[count:]


def exchange(blocks, axis, order):
    count = len(blocks)
    out = []
    for s, block in zip(order, blocks):
        perm = [(i, (i + s) % count) for i in range(count)]
        out.append(lax.ppermute(block, axis, perm) if s else block)
    return out


def gather_positions(me, blocks, spot, count, order):
    outer_here = blocks[0].shape[0] // spot.shape[1]
    for j, s in enumerate(order(count)):
        src = lax.rem(me + count - s, count)
        spot[pl.ds(src * outer_here, outer_here)] = blocks[j][...].reshape(outer_here, *spot.shape[1:])


def halves(tile):
    tile = tile.astype(F32)
    width = tile.shape[-1]
    return jnp.concatenate(
        [tile[..., at : at + SUB, :].reshape(-1, width).astype(BF16) for at in (0, SUB)], axis=1
    )


def joined(value, lead):
    width = value.shape[1] // 2
    parts = [value[:, at : at + width].reshape(*lead, SUB, width) for at in (0, width)]
    return jnp.concatenate(parts, axis=len(lead)).astype(BF16)


def for_each(count, body):
    if count <= 32:
        for i in range(count):
            body(i)
    else:
        lax.fori_loop(0, count, lambda i, c: (body(i), c)[1], 0, unroll=4 if count % 4 == 0 else 1)


def forward_first(first_ref, spot, mixed):
    outer, inner, _ = spot.shape

    def body(i):
        rows = pl.ds(i * 2 * SUB, 2 * SUB)
        value = jnp.dot(first_ref[...], halves(spot[:, rows, :]), preferred_element_type=F32)
        mixed[:, :, rows, :] = joined(value, (outer, 2))

    for_each(inner // (2 * SUB), body)


def filter_kernel(idx_ref, first_ref, mid_hbm, back_hbm, *refs, count):
    blocks, (out_ref, mid_ref, back_ref, spot, mixed, sems) = refs[:count], refs[count:]
    outer, _, inner, width = mixed.shape
    parts = sems.shape[0] - 1
    cuts = [outer * p // parts for p in range(parts + 1)]
    spans = [pl.ds(lo, hi - lo) for lo, hi in zip(cuts, cuts[1:])]
    copies = [pltpu.make_async_copy(mid_hbm.at[at], mid_ref.at[at], sems.at[p]) for p, at in enumerate(spans)]
    copies.append(pltpu.make_async_copy(back_hbm, back_ref, sems.at[parts]))
    for copy in copies:
        copy.start()
    gather_positions(idx_ref[0], blocks, spot, count, filter_order)
    forward_first(first_ref, spot, mixed)

    for p in range(parts):
        copies[p].wait()

        def body(k):
            k = k + cuts[p]
            out_ref[k] = jnp.dot(
                mid_ref[k], mixed[k].reshape(2 * inner, width), preferred_element_type=F32
            ).astype(BF16)

        for_each(cuts[p + 1] - cuts[p], body)
    copies[parts].wait()


def conv_kernel(idx_ref, first_ref, mid_ref, back_ref, last_ref, filt_ref, *refs, count):
    blocks, outs, (spot, mixed) = refs[:count], refs[count : 2 * count], refs[2 * count :]
    me = idx_ref[0]
    gather_positions(me, blocks, spot, count, gated_order)
    forward_first(first_ref, spot, mixed)
    outer, _, inner, width = mixed.shape

    def middle(k):
        spec = jnp.dot(mid_ref[k], mixed[k].reshape(2 * inner, width), preferred_element_type=F32)
        filt = filt_ref[k].astype(F32)
        re, im = spec[:inner], spec[inner:]
        fre, fim = filt[:inner], filt[inner:]
        prod = jnp.concatenate([re * fre - im * fim, re * fim + im * fre], axis=0).astype(BF16)
        turned = jnp.dot(back_ref[k], prod, preferred_element_type=F32)
        mixed[k] = turned.astype(BF16).reshape(2, inner, width)

    for_each(outer, middle)

    def ending(i):
        rows = pl.ds(i * 2 * SUB, 2 * SUB)
        value = jnp.dot(last_ref[...], halves(mixed[:, :, rows, :]), preferred_element_type=F32)
        spot[:, rows, :] = joined(value, (outer,))

    for_each(inner // (2 * SUB), ending)
    here = outer // count
    for j, s in enumerate(conv_order(count)):
        dst = lax.rem(me + s, count)
        outs[j][...] = spot[pl.ds(dst * here, here)].reshape(here * inner, width)


def hidden_rows(idx_ref, gain_ref, gate_ref, key_ref, value_ref, blocks, out_ref, at):
    me, count = idx_ref[0], len(blocks)
    width = blocks[0].shape[1]
    rows = slice(at, at + out_ref.shape[0])
    for j, s in enumerate(conv_order(count)):
        src = lax.rem(me + count - s, count)
        cols = pl.ds(pl.multiple_of(src * width, width), width)
        gated = (key_ref[rows, cols].astype(F32) * value_ref[rows, cols].astype(F32)).astype(BF16).astype(F32)
        total = blocks[j][rows, :].astype(F32) + gain_ref[:, cols] * gated
        out_ref[:, cols] = (gate_ref[rows, cols].astype(F32) * total).astype(BF16)


def times_columns(hid_ref, weight_ref, part_ref, extra_ref=None):
    width = part_ref.shape[1]
    tile = min(256, width)
    for j in range(width // tile):
        cols = slice(j * tile, (j + 1) * tile)
        value = jnp.dot(hid_ref[...], weight_ref[:, cols], preferred_element_type=F32)
        if extra_ref is not None:
            value = value + extra_ref[:, cols].astype(F32)
        part_ref[:, cols] = value.astype(part_ref.dtype)


def rows_kernel(idx_ref, gain_ref, gate_ref, key_ref, value_ref, *refs, at, others, more):
    weights, refs = refs[:others], refs[others:]
    if more:
        own_ref, first_ref, *refs = refs
        *refs, own_first = refs
    *blocks, hid_ref, part_ref = refs
    if more:
        times_columns(first_ref, own_ref, own_first)
    hidden_rows(idx_ref, gain_ref, gate_ref, key_ref, value_ref, blocks, hid_ref, at)
    for j, weight_ref in enumerate(weights):
        cols = weight_ref.shape[1]
        times_columns(hid_ref, weight_ref, part_ref.at[:, j * cols : (j + 1) * cols])


def hidden_products(arrays, weights, blocks, at, rows, more=()):
    total, channels = arrays[2].shape
    columns = weights[0].shape[1]
    pinned = [pltpu.with_memory_space_constraint(w, pltpu.VMEM) for w in (*weights, *more)]
    limit = 2 * (len(pinned) + 1) * channels * columns + 12 * total * channels + 8 * total * columns
    outs = [pltpu.VMEM((rows, channels), BF16), pltpu.VMEM((rows, len(weights) * columns), BF16)]
    if more:
        outs.append(pltpu.VMEM((more[1].shape[0], columns), BF16))
    return pl.pallas_call(
        functools.partial(rows_kernel, at=at, others=len(weights), more=bool(more)),
        out_shape=outs,
        in_specs=[SMEM] + [VMEM] * (4 + len(pinned) + len(blocks)),
        out_specs=[VMEM] * len(outs),
        compiler_params=params(limit),
        cost_estimate=pl.CostEstimate(flops=4 * rows * channels * columns, bytes_accessed=limit, transcendentals=0),
    )(*arrays, *pinned, *blocks)


def own_kernel(hid_ref, weight_ref, crossed_ref, out_ref, *, at):
    times_columns(hid_ref, weight_ref, out_ref, crossed_ref.at[:, at : at + out_ref.shape[1]])


def own_product(hidden, weight, crossed, at=0):
    rows, channels = hidden.shape
    columns = weight.shape[1]
    return pl.pallas_call(
        functools.partial(own_kernel, at=at),
        out_shape=pltpu.VMEM((rows, columns), BF16),
        in_specs=[VMEM] * 3,
        out_specs=VMEM,
        compiler_params=params(2 * channels * columns + 4 * rows * channels + 8 * rows * columns),
        cost_estimate=pl.CostEstimate(
            flops=2 * rows * channels * columns, bytes_accessed=2 * channels * columns, transcendentals=0
        ),
    )(*(pltpu.with_memory_space_constraint(a, pltpu.VMEM) for a in (hidden, weight, crossed)))


def add_kernel(own_ref, other_ref, out_ref):
    other = other_ref[:, : own_ref.shape[1]].astype(F32)
    out_ref[...] = (own_ref[...].astype(F32) + other).astype(BF16)


def add(own, other):
    return pl.pallas_call(
        add_kernel,
        out_shape=pltpu.VMEM(own.shape, BF16),
        in_specs=[VMEM] * 2,
        out_specs=VMEM,
        compiler_params=params(4 * own.size + 2 * other.size),
        cost_estimate=pl.CostEstimate(flops=own.size, bytes_accessed=6 * own.size, transcendentals=0),
    )(own, pltpu.with_memory_space_constraint(other, pltpu.VMEM))


def last_kernel(weight_ref, *refs, pieces, at):
    hids, extras, parts = refs[:pieces], refs[pieces : 2 * pieces], refs[2 * pieces :]
    for hid_ref, extra_ref, part_ref in zip(hids, extras, parts):
        times_columns(hid_ref, weight_ref, part_ref, extra_ref.at[:, at : at + part_ref.shape[1]])


def last_products(hidden, weight, crossed, at):
    channels, columns = weight.shape
    rows = sum(h.shape[0] for h in hidden)
    return pl.pallas_call(
        functools.partial(last_kernel, pieces=len(hidden), at=at),
        out_shape=[pltpu.VMEM((h.shape[0], columns), F32) for h in hidden],
        in_specs=[VMEM] * (1 + 2 * len(hidden)),
        out_specs=[VMEM] * len(hidden),
        compiler_params=params(2 * weight.size + 2 * rows * channels + 2 * sum(c.size for c in crossed) + 4 * rows * columns),
        cost_estimate=pl.CostEstimate(flops=0, bytes_accessed=channels, transcendentals=0),
    )(*(pltpu.with_memory_space_constraint(a, pltpu.VMEM) for a in (weight, *hidden, *crossed)))


def finish_kernel(*refs, at, terms):
    values, (out_ref, held, sems) = refs[:terms], refs[-3:]
    parts = sems.shape[0]
    rows = held.shape[0] // parts
    copies = []
    for p in range(parts):
        block = pl.ds(p * rows, rows)
        total = values[0][block, :]
        for value in values[1:]:
            total = total + value[block, :].astype(F32)
        held[block, :] = total.astype(BF16)
        copies.append(pltpu.make_async_copy(held.at[block, :], out_ref.at[pl.ds(at + p * rows, rows), :], sems.at[p]))
        copies[-1].start()
    for copy in copies:
        copy.wait()


def finish(values, at, rows, buffer):
    here, columns = values[0].shape
    aliased = [] if buffer is None else [buffer]
    return pl.pallas_call(
        functools.partial(finish_kernel, at=at, terms=len(values)),
        out_shape=jax.ShapeDtypeStruct((rows, columns), BF16),
        in_specs=[VMEM] * len(values) + [HBM] * len(aliased),
        out_specs=HBM,
        scratch_shapes=[pltpu.VMEM((here, columns), BF16), pltpu.SemaphoreType.DMA((4 if here % 64 == 0 else 1,))],
        input_output_aliases={len(values): 0} if aliased else {},
        compiler_params=params(4 * here * columns * (len(values) + 2)),
        cost_estimate=pl.CostEstimate(flops=0, bytes_accessed=columns, transcendentals=0),
    )(*(pltpu.with_memory_space_constraint(v, pltpu.VMEM) for v in values), *aliased)


def local(gate_q, key_k, value_v, long_filter, skip_gain, out_weight):
    rows, channels = key_k.shape
    count = lax.axis_size("ctx")
    groups = lax.axis_size("ch")
    chips = groups // 2
    total = rows * count
    inner = next(n for n in range(128, 0, -16) if rows % n == 0)
    outer = total // inner
    width = channels // count
    lanes = -(-width // 128) * 128
    idx = lax.axis_index("ctx").astype(jnp.int32).reshape(1)
    first, mid, back, last = tables(total, inner)
    spot = pltpu.VMEM((outer, inner, width), BF16)
    mixed = pltpu.VMEM((outer, 2, inner, width), BF16)
    signal = 2 * total * lanes
    table = 2 * (first.size + mid.size)

    here = lax.axis_index("ch").astype(jnp.int32)
    chip, core = here // 2, here % 2

    def group_of(step, which):
        return lax.rem(chip + step, chips) * 2 + which

    filter_in = exchange(filter_slices(idx, long_filter, count, filter_order), "ctx", filter_order(count))
    steps = list(range(1, chips)) + [0]
    order = jnp.stack([group_of(step, which) for which in (1 - core, core) for step in steps])
    slices, weights = gated_slices(idx, key_k, value_v, count, order, out_weight, groups)
    gated_in = exchange(slices, "ctx", gated_order(count))
    spectrum, mid, back = pl.pallas_call(
        functools.partial(filter_kernel, count=count),
        out_shape=[
            jax.ShapeDtypeStruct((outer, 2 * inner, width), BF16),
            jax.ShapeDtypeStruct(mid.shape, BF16),
            jax.ShapeDtypeStruct(back.shape, BF16),
        ],
        in_specs=[SMEM, VMEM, HBM, HBM] + [VMEM] * count,
        out_specs=[VMEM] * 3,
        scratch_shapes=[spot, mixed, pltpu.SemaphoreType.DMA((5,))],
        compiler_params=params(2 * table + 6 * signal),
        cost_estimate=pl.CostEstimate(flops=3 * 10**9, bytes_accessed=8 * 10**6, transcendentals=0),
    )(
        idx,
        first,
        pltpu.with_memory_space_constraint(mid, pltpu.HBM),
        pltpu.with_memory_space_constraint(back, pltpu.HBM),
        *filter_in,
    )
    conv_out = pl.pallas_call(
        functools.partial(conv_kernel, count=count),
        out_shape=[jax.ShapeDtypeStruct((rows, width), BF16)] * count,
        in_specs=[SMEM] + [VMEM] * (5 + count),
        out_specs=[VMEM] * count,
        scratch_shapes=[spot, mixed],
        compiler_params=params(2 * table + 7 * signal),
        cost_estimate=pl.CostEstimate(flops=6 * 10**9, bytes_accessed=12 * 10**6, transcendentals=0),
    )(idx, first, mid, back, last, spectrum, *gated_in)
    conv_in = exchange(conv_out, "ctx", conv_order(count))

    swap = [(i, i ^ 1) for i in range(groups)]
    lead = rows // 32 * 16

    def to_chip(part, step):
        return lax.ppermute(part, "ch", [(i, (i + 2 * step) % groups) for i in range(groups)])

    gain = skip_gain[None, :]
    if width % 128:
        conv = jnp.zeros((rows, channels), BF16)
        for j, s in enumerate(conv_order(count)):
            src = lax.rem(idx[0] + count - s, count)
            conv = lax.dynamic_update_slice_in_dim(conv, conv_in[j], src * width, 1)
        idx, conv_in = jnp.zeros_like(idx), [conv]
    arrays = [idx, gain, gate_q, key_k, value_v]
    others, owns = weights[:chips], weights[chips:]
    columns = owns[0].shape[1]
    hid_first, part_first = hidden_products(arrays, others, conv_in, 0, lead)
    crossed = [lax.ppermute(part_first, "ch", swap)]
    hid_rest, part_rest, sums = hidden_products(arrays, others, conv_in, lead, rows - lead, (owns[0], hid_first))
    crossed.append(lax.ppermute(part_rest, "ch", swap))
    arrived = [[to_chip(add(sums, crossed[0]), 1)], [to_chip(own_product(hid_rest, owns[0], crossed[1]), 1)]]
    for j, step in enumerate(steps[1:-1]):
        for got, hid, cross in zip(arrived, (hid_first, hid_rest), crossed):
            got.append(to_chip(own_product(hid, owns[j + 1], cross, (j + 1) * columns), step))
    last = (chips - 1) * columns
    sums = last_products((hid_first, hid_rest), owns[-1], crossed, last)
    out = finish([sums[0]] + arrived[0], 0, rows, None)
    return finish([sums[1]] + arrived[1], lead, rows, out)


def solution(mesh):
    placed = (
        P("ctx", "ch"),
        P("ctx", "ch"),
        P("ctx", "ch"),
        P("ctx", "ch"),
        P("ch"),
        P("ch", None),
    )
    return jax.shard_map(
        local, mesh=mesh, in_specs=placed, out_specs=P("ctx", "ch"), check_vma=False
    )
```
